512 devices in a mesh: image: 16 (over y, z_hi, core), space: 32 (over x, z_lo).
Axes of the slice: x: 4, y: 4, z: 16 (z_hi: 2, z_lo: 8; z = z_hi * 8 + z_lo), core: 2. Of those that a mesh axis runs over, the one named last changes fastest.
Arguments:
- positions: float32 [16, 3, 4096], P('image', None, 'space'), may hold values from -4 to 36
- velocity: float32 [16, 3, 4096], P('image', None, 'space'), may hold values from -3 to 3
- embed: bfloat16 [4096, 128], P('space'), may hold values from -6 to 6
- neighbours: int32 [4096, 32], P('space'), may hold values from 0 to 383
- send_up: int32 [4096], P('space'), may hold values from 0 to 127
- send_down: int32 [4096], P('space'), may hold values from 0 to 127
- climb: int32 [16], P('image'), may hold values from 0 to 1
- reset: int32 [16], P('image'), may hold values from 0 to 1
- filter_in: float32 [2, 16, 128], replicated, may hold values from -1.5 to 1.5
- filter_out: bfloat16 [2, 128, 128], replicated, may hold values from -0.5 to 0.5
- update_weight: bfloat16 [2, 128, 128], replicated, may hold values from -0.5 to 0.5
- readout: float32 [128], replicated, may hold values from -0.5 to 0.5
- spring: float32 [], replicated, may hold values from 2 to 20
- time_step: float32 [], replicated, may hold values from 0.05 to 0.2
- mixing: float32 [], replicated, may hold values from 0.05 to 0.3
Outputs:
- new_positions: float32 [16, 3, 4096], P('image', None, 'space')
- new_velocity: float32 [16, 3, 4096], P('image', None, 'space')
- energies: float32 [16], P('image')
The draws below stay inside these ranges and needn't reach their ends.
All inputs are finite; a program needn't handle non-finite values.
Results may differ from the reference program's by a relative error of at most 0.0095.
Values may be sent and summed in bfloat16 or wider, within the bound.
No kernel may reach another device: no remote copies, remote signals or barrier semaphores. Data moves between devices by JAX's collectives and lax.ppermute only.
A program may use at most 64 MiB of HBM per device.

```python
import math
import jax
import jax.numpy as jnp
from jax import lax

CHANNELS = 128
BASIS = 16
NEIGH_COUNT = 32
LAYERS = 2
ATOM_DEV = 128
GHOST_DEV = 128
IMAGES = 16
ATOMS = 4096
GHOST_ALL = 4096
N_SPACE = 32


def draw_positions(key, part):
    key_base, key_head, key_step, key_noise = jax.random.split(key, 4)
    atom_ids = lax.iota(jnp.int32, ATOMS)
    slab = (atom_ids // ATOM_DEV).astype(jnp.float32)
    fraction = slab / (N_SPACE - 1)
    first_axis = (lax.iota(jnp.int32, 3) == 0).astype(jnp.float32)[:, None]
    base = jax.random.uniform(key_base, (3, ATOMS), jnp.float32) + first_axis * slab[None, :]
    heading = 0.25 * jnp.clip(jax.random.normal(key_head, (3, ATOMS), jnp.float32), -3.0, 3.0)
    progress = (lax.iota(jnp.float32, IMAGES) + 0.4 * jax.random.uniform(key_step, (IMAGES,), jnp.float32)) * (0.8 / IMAGES)
    ramp = 0.4 + 3.6 * fraction
    noise = 0.04 * jnp.clip(jax.random.normal(key_noise, (IMAGES, 3, ATOMS), jnp.float32), -3.5, 3.5)
    return base[None] + ramp[None, None, :] * (progress[:, None, None] * heading[None] + noise)


def place_ends(entries, rng, least, high):
    spot = [jax.random.randint(jax.random.fold_in(rng, axis), (), 0, length) for axis, length in enumerate(entries.shape)]
    widest = entries.shape.index(max(entries.shape))
    neighbour = spot[:widest] + [(spot[widest] + 1) % entries.shape[widest]] + spot[widest + 1:]
    return entries.at[tuple(spot)].set(least).at[tuple(neighbour)].set(high)


def shard_levels(key, dims, cuts, least, largest):
    level = 1.0
    for dim, parts in cuts:
        heights = jax.random.uniform(jax.random.fold_in(jax.random.fold_in(key, 6), dim), (parts,), jnp.float32, least / len(cuts), largest / len(cuts))
        level = level * jnp.repeat(jnp.exp(heights), dims[dim] // parts).reshape((-1,) + (1,) * (len(dims) - 1 - dim))
    return level


def centred(key, shape, scale, most, shards=(), held_as=jnp.bfloat16):
    loudness = shard_levels(key, shape, shards, -0.22, 0.18) if shards else 1.0
    drawn = jax.random.normal(key, shape, jnp.float32) * scale * loudness
    return jnp.minimum(jnp.maximum(drawn, -most), most).astype(held_as)


def setup_inputs(seed: int = 0) -> dict:
    key_of = jax.random.split(jax.random.key(seed), 16)
    positions = draw_positions(jax.random.fold_in(key_of[15], 71), 0)
    velocity = centred(key_of[1], (IMAGES, 3, ATOMS), 0.5, 3.0, ((0, 16), (2, 32)), jnp.float32)
    embed = centred(key_of[2], (ATOMS, CHANNELS), 1.0, 6.0, ((0, 32),))
    neighbours = place_ends(jax.random.randint(key_of[3], (ATOMS, NEIGH_COUNT), 0, ATOM_DEV + 2 * GHOST_DEV), jax.random.fold_in(key_of[3], 1), 0, (ATOM_DEV + 2 * GHOST_DEV) - 1).astype(jnp.int32)
    send_up = place_ends(jax.random.randint(key_of[4], (GHOST_ALL,), 0, ATOM_DEV), jax.random.fold_in(key_of[4], 1), 0, ATOM_DEV - 1).astype(jnp.int32)
    send_down = place_ends(jax.random.randint(key_of[5], (GHOST_ALL,), 0, ATOM_DEV), jax.random.fold_in(key_of[5], 1), 0, ATOM_DEV - 1).astype(jnp.int32)
    climb = place_ends(jax.random.randint(key_of[6], (IMAGES,), 0, 2), jax.random.fold_in(key_of[6], 1), 0, 1).astype(jnp.int32)
    reset = place_ends(jax.random.randint(key_of[7], (IMAGES,), 0, 2), jax.random.fold_in(key_of[7], 1), 0, 1).astype(jnp.int32)
    filter_in = centred(key_of[8], (LAYERS, BASIS, CHANNELS), BASIS ** -0.5, 1.5, (), jnp.float32)
    filter_out = centred(key_of[9], (LAYERS, CHANNELS, CHANNELS), CHANNELS ** -0.5, 0.5)
    update_weight = centred(key_of[10], (LAYERS, CHANNELS, CHANNELS), CHANNELS ** -0.5, 0.5)
    readout = centred(key_of[11], (CHANNELS,), CHANNELS ** -0.5, 0.5, (), jnp.float32)
    spring = jnp.clip(jnp.exp(jax.random.uniform(key_of[12], (), jnp.float32, math.log(2.0), math.log(20.0))), 2.0, 20.0)
    time_step = jnp.clip(jax.random.uniform(key_of[13], (), jnp.float32, 0.05, 0.2), 0.05, 0.2)
    mixing = jnp.clip(jax.random.uniform(key_of[14], (), jnp.float32, 0.05, 0.3), 0.05, 0.3)
    return dict(positions=positions, velocity=velocity, embed=embed, neighbours=neighbours, send_up=send_up, send_down=send_down, climb=climb, reset=reset, filter_in=filter_in, filter_out=filter_out, update_weight=update_weight, readout=readout, spring=spring, time_step=time_step, mixing=mixing)


EPSILON = 1e-06
BASIS_WIDTH = 0.6
BASIS_REACH = 6.0
HIGHEST = lax.Precision.HIGHEST

def silu_grad(values):
    sigmoid = jax.nn.sigmoid(values)
    return sigmoid * (1.0 + values * (1.0 - sigmoid))

def radial(sq_dist, basis_count):
    centres = lax.iota(jnp.float32, basis_count) * (BASIS_REACH / (basis_count - 1))
    scaled = (sq_dist[None, :] - centres[:, None]) / BASIS_WIDTH
    radial_vals = jnp.exp(-scaled * scaled)
    radial_slope = radial_vals * (-2.0 / BASIS_WIDTH) * scaled
    return (radial_vals, radial_slope)

def pair_filter(radial_vals, weight_in, weight_out):
    pre_act = lax.dot_general(radial_vals, weight_in, (((0,), (0,)), ((), ())), precision=HIGHEST, preferred_element_type=jnp.float32)
    activated = jax.nn.silu(pre_act).astype(jnp.bfloat16)
    filter_vals = jnp.dot(activated, weight_out, preferred_element_type=jnp.float32)
    return (pre_act, filter_vals)

def gather_message(filter_vals, source_rows, per_atom):
    product = filter_vals * source_rows.astype(jnp.float32)
    return lax.optimization_barrier(jnp.sum(product.reshape(-1, per_atom, product.shape[1]), axis=1))

def filter_back(grad_msg, source_rows, radial_vals, weight_in, weight_out, per_atom):
    pre_act, filter_vals = pair_filter(radial_vals, weight_in, weight_out)
    repeated = jnp.repeat(grad_msg, per_atom, axis=0)
    grad_filter = (repeated * source_rows.astype(jnp.float32)).astype(jnp.bfloat16)
    grad_source = filter_vals * repeated
    grad_act = lax.dot_general(grad_filter, weight_out, (((1,), (1,)), ((), ())), preferred_element_type=jnp.float32)
    grad_pre = grad_act * silu_grad(pre_act)
    grad_radial = lax.dot_general(weight_in, grad_pre, (((1,), (1,)), ((), ())), precision=HIGHEST, preferred_element_type=jnp.float32)
    return (grad_source, grad_radial)

def image_terms(coords, embed, target, offset, filter_in, filter_out, update_weight, readout):
    per_atom = NEIGH_COUNT
    first_axis = (lax.iota(jnp.int32, 3) == 0).astype(jnp.float32)[:, None]
    flat_ids = target.reshape(-1)
    neighbour_pos = coords[:, flat_ids] + offset.reshape(-1)[None, :] * first_axis
    pair_vec = neighbour_pos - jnp.repeat(coords, per_atom, axis=1)
    sq_dist = lax.optimization_barrier(jnp.sum(pair_vec * pair_vec, axis=0))
    radial_vals, radial_slope = radial(sq_dist, BASIS)
    embed_rows = embed[flat_ids]
    pre_one, filter_one = pair_filter(radial_vals, filter_in[0], filter_out[0])
    message_one = gather_message(filter_one, embed_rows, per_atom).astype(jnp.bfloat16)
    update_one = jnp.dot(message_one, update_weight[0], preferred_element_type=jnp.float32)
    hidden = (embed.astype(jnp.float32) + jax.nn.silu(update_one)).astype(jnp.bfloat16)
    hidden_rows = hidden[flat_ids]
    pre_two, filter_two = pair_filter(radial_vals, filter_in[1], filter_out[1])
    message_two = gather_message(filter_two, hidden_rows, per_atom).astype(jnp.bfloat16)
    update_two = jnp.dot(message_two, update_weight[1], preferred_element_type=jnp.float32)
    energy = jnp.sum(jnp.dot(jax.nn.silu(update_two), readout, precision=HIGHEST))
    grad_update_two = (silu_grad(update_two) * readout[None, :]).astype(jnp.bfloat16)
    grad_msg_two = lax.dot_general(grad_update_two, update_weight[1], (((1,), (1,)), ((), ())), preferred_element_type=jnp.float32)
    grad_source_two, grad_radial_two = filter_back(grad_msg_two, hidden_rows, radial_vals, filter_in[1], filter_out[1], per_atom)
    grad_hidden = jnp.zeros(hidden.shape, jnp.float32).at[flat_ids].add(grad_source_two)
    grad_update_one = (grad_hidden * silu_grad(update_one)).astype(jnp.bfloat16)
    grad_msg_one = lax.dot_general(grad_update_one, update_weight[0], (((1,), (1,)), ((), ())), preferred_element_type=jnp.float32)
    grad_source_one, grad_radial_one = filter_back(grad_msg_one, embed_rows, radial_vals, filter_in[0], filter_out[0], per_atom)
    grad_sq = lax.optimization_barrier(jnp.sum((grad_radial_one + grad_radial_two) * radial_slope, axis=0))
    pair_grad = 2.0 * grad_sq[None, :] * pair_vec
    gradient = jnp.zeros(coords.shape, jnp.float32).at[:, flat_ids].add(pair_grad)
    gradient = gradient - lax.optimization_barrier(jnp.sum(pair_grad.reshape(3, -1, per_atom), axis=2))
    return (energy, -gradient)

def image_sum(values):
    return lax.optimization_barrier(jnp.sum(values, axis=(1, 2)))[:, None, None]

def reference(positions, velocity, embed, neighbours, send_up, send_down, climb, reset, filter_in, filter_out, update_weight, readout, spring, time_step, mixing):
    atom_ids = lax.iota(jnp.int32, ATOMS)
    domain = (atom_ids // ATOM_DEV)[:, None]
    lower_dom = (domain + N_SPACE - 1) % N_SPACE
    upper_dom = (domain + 1) % N_SPACE
    low_slot = jnp.clip(neighbours - ATOM_DEV, 0, GHOST_DEV - 1)
    high_slot = jnp.clip(neighbours - ATOM_DEV - GHOST_DEV, 0, GHOST_DEV - 1)
    from_low = lower_dom * ATOM_DEV + send_up[(lower_dom * GHOST_DEV + low_slot).astype(jnp.int32)]
    from_high = upper_dom * ATOM_DEV + send_down[(upper_dom * GHOST_DEV + high_slot).astype(jnp.int32)]
    own_ids = domain * ATOM_DEV + neighbours
    is_local = neighbours < ATOM_DEV
    is_low = (neighbours >= ATOM_DEV) & (neighbours < ATOM_DEV + GHOST_DEV)
    is_high = neighbours >= ATOM_DEV + GHOST_DEV
    target = jnp.where(is_local, own_ids, jnp.where(is_low, from_low, from_high)).astype(jnp.int32)
    offset = jnp.where(is_low & (domain == 0), -1.0, 0.0) + jnp.where(is_high & (domain == N_SPACE - 1), 1.0, 0.0)
    offset = (offset * N_SPACE).astype(jnp.float32)

    def one_image(coords):
        return image_terms(coords, embed, target, offset, filter_in, filter_out, update_weight, readout)
    energies, forces = lax.map(one_image, positions)
    zero_image = jnp.zeros_like(positions[:1])
    previous = jnp.concatenate([zero_image, positions[:-1]], axis=0)
    following = jnp.concatenate([positions[1:], zero_image], axis=0)
    ahead_vec = following - positions
    behind = positions - previous
    ahead_norm = jnp.sqrt(image_sum(ahead_vec * ahead_vec) + EPSILON)
    behind_norm = jnp.sqrt(image_sum(behind * behind) + EPSILON)
    tangent = ahead_vec / ahead_norm + behind / behind_norm
    unit_tangent = tangent / jnp.sqrt(image_sum(tangent * tangent) + EPSILON)
    parallel = image_sum(forces * unit_tangent)
    image_index = lax.iota(jnp.int32, IMAGES)[:, None, None]
    movable = (image_index > 0) & (image_index < IMAGES - 1)
    climbing = climb[:, None, None] > 0
    spring_part = spring * (ahead_norm - behind_norm)
    band_force = jnp.where(climbing, forces - 2.0 * parallel * unit_tangent, forces - parallel * unit_tangent + spring_part * unit_tangent)
    band_force = jnp.where(movable, band_force, 0.0)
    force_norm = jnp.sqrt(jnp.sum(band_force * band_force) + EPSILON)
    speed_norm = jnp.sqrt(jnp.sum(jnp.where(movable, velocity * velocity, 0.0)) + EPSILON)
    mixed = (1.0 - mixing) * velocity + mixing * (speed_norm / force_norm) * band_force
    kept_speed = jnp.where(reset[:, None, None] > 0, 0.0, mixed)
    new_velocity = jnp.where(movable, kept_speed + time_step * band_force, 0.0)
    new_positions = positions + time_step * new_velocity
    return (new_positions, new_velocity, energies)
```

```python
import jax
import jax.numpy as jnp
from jax import lax
from jax.experimental import pallas as pl
from jax.experimental.pallas import tpu as pltpu
from jax.sharding import PartitionSpec as P

EPSILON = 1e-06
BASIS_WIDTH = 0.6
BASIS_REACH = 6.0
BASIS = 16
IMAGES = 16
DOMAINS = 32
ATOMS = 128
CHANNELS = 128
SLOTS = 32
PAIRS = ATOMS * SLOTS
CHUNK = 512
PER_CHUNK = CHUNK // ATOMS
CHUNKS = PAIRS // CHUNK
EXT = 3 * ATOMS
AXES = ("image", "space")
F32 = jnp.float32
BF16 = jnp.bfloat16

ROW_POS = 128
ROW_AUX = 152
ROW_NEAR = 160
PACK_ROWS = 192
HALO_ROWS = 160


def device_at(x, y, z, core):
    return ((y * 2 + z // 8) * 2 + core) * DOMAINS + x * 8 + z % 8


def home(image, domain):
    return image * DOMAINS + domain


def worker(image, domain):
    x, rest = divmod(domain, 8)
    pair, core = divmod(rest, 2)
    return device_at(x, pair if x % 2 == 0 else 3 - pair, image, core)


CELLS = [(i, d) for i in range(IMAGES) for d in range(DOMAINS)]
TO_WORKER = [(home(i, d), worker(i, d)) for i, d in CELLS]
TO_HOME = [(worker(i, d), home(i, d)) for i, d in CELLS]
SWAP_A = [(worker(i, d), worker(i, d ^ 1)) for i, d in CELLS]
SWAP_B = [(worker(i, d), worker(i, (d + 1) % DOMAINS if d % 2 else (d - 1) % DOMAINS)) for i, d in CELLS]
IMAGE_UP = [(worker(i, d), worker(i + 1, d)) for i, d in CELLS if i + 1 < IMAGES]
IMAGE_DOWN = [(worker(i + 1, d), worker(i, d)) for i, d in CELLS if i + 1 < IMAGES]
LAYERS = [[worker(i, d) for d in range(DOMAINS)] for i in range(IMAGES)]
COLUMNS = [[worker(i, d) for i in range(IMAGES)] for d in range(DOMAINS)]


def move(values, pairs):
    return lax.ppermute(values, AXES, pairs)


def place():
    image, space = lax.axis_index("image"), lax.axis_index("space")
    x, y = lax.shift_right_logical(space, 3), lax.shift_right_logical(image, 2)
    layer = ((image & 2) << 2) + (space & 7)
    pair = jnp.where((x & 1) == 0, y, 3 - y)
    return image, layer, x * 8 + pair * 2 + (image & 1)


def dot(a, b):
    return jnp.dot(a, b, preferred_element_type=F32)


def dot_nt(a, b):
    return lax.dot_general(a, b, (((1,), (1,)), ((), ())), preferred_element_type=F32)


def gate(v):
    return 0.5 * jnp.tanh(0.5 * v) + 0.5


def halves(v):
    high = v.astype(BF16)
    return high, (v - high.astype(F32)).astype(BF16)


def thirds(v):
    high = v.astype(BF16)
    rest = v - high.astype(F32)
    middle = rest.astype(BF16)
    return high, middle, (rest - middle.astype(F32)).astype(BF16)


def centres():
    step = BASIS_REACH / (BASIS - 1)
    return lax.broadcasted_iota(jnp.int32, (BASIS, CHUNK), 0).astype(F32) * step


def stacked(v):
    high, low = halves(v)
    return jnp.concatenate([high, low, high], axis=0)


def chunk(c):
    return pl.ds(c * CHUNK, CHUNK)


def fold(v):
    total = v[:, :ATOMS]
    for k in range(1, PER_CHUNK):
        total = total + v[:, k * ATOMS : (k + 1) * ATOMS]
    return total


def spread(v):
    return jnp.concatenate([v] * PER_CHUNK, axis=1)


def coords_of(block):
    b = block[ROW_POS : ROW_POS + 24].astype(F32)
    return b[0:8] + b[8:16] + b[16:24]


def pack_kernel(pos, embed, near, up, down, climb, out):
    out[0:CHANNELS, :] = embed[...].astype(F32).T.astype(BF16)
    zeros = jnp.zeros((5, ATOMS), F32)
    parts = [jnp.concatenate([p.astype(F32), zeros], axis=0) for p in thirds(pos[0])]
    level = jnp.full((1, ATOMS), climb[0].astype(F32) * (1.0 / DOMAINS), F32)
    aux = jnp.concatenate([level, up[...].astype(F32), down[...].astype(F32), zeros], axis=0)
    out[ROW_POS:ROW_NEAR, :] = jnp.concatenate(parts + [aux], axis=0).astype(BF16)
    slots = near[...].astype(F32) - float(ATOMS)
    square = jnp.concatenate([slots, jnp.zeros((ATOMS, ATOMS - SLOTS), F32)], axis=1)
    out[ROW_NEAR:PACK_ROWS, :] = square.T[:SLOTS].astype(BF16)


def weights_kernel(after, filter_in, filter_out, update, readout, in_t, out_t, update_t, read):
    for l in range(2):
        rows = pl.ds(l * 128, 128)
        high, low = halves(filter_in[l])
        filler = jnp.zeros((128 - 3 * BASIS, CHANNELS), F32)
        tall = jnp.concatenate(
            [high.astype(F32), high.astype(F32), low.astype(F32), filler], axis=0
        )
        in_t[rows, :] = tall.T.astype(BF16)
        out_t[rows, :] = filter_out[l].astype(F32).T.astype(BF16)
        update_t[rows, :] = update[l].astype(F32).T.astype(BF16)
    read[...] = jnp.broadcast_to(readout[...], (CHANNELS, ATOMS)).T


def lists_kernel(pack, list_a, list_b, send_a, send_b):
    _, _, domain = place()
    even = (domain & 1) == 0
    aux = pack[ROW_AUX : ROW_AUX + 8, :].astype(F32)
    up, down = aux[1:2], aux[2:3]
    rows = lax.broadcasted_iota(jnp.int32, (ATOMS, ATOMS), 0).astype(F32)
    block = pack[0:HALO_ROWS, :]
    for ids, chosen, send in (
        (jnp.where(even, up, down), list_a, send_a),
        (jnp.where(even, down, up), list_b, send_b),
    ):
        hot = jnp.where(rows == ids, 1.0, 0.0).astype(BF16)
        chosen[...] = hot
        send[...] = dot(block, hot).astype(BF16)


def slots_kernel(pack, hot):
    _, _, domain = place()
    even = (domain & 1) == 0
    slots = pack[ROW_NEAR:PACK_ROWS, :].astype(F32)
    swapped = jnp.where(slots < 0.0, slots, jnp.where(slots < 128.0, slots + 128.0, slots - 128.0))
    slots = jnp.where(even, swapped, slots)
    rows = lax.broadcasted_iota(jnp.int32, (EXT, ATOMS), 0).astype(F32) - float(ATOMS)
    for k in range(SLOTS):
        hot[:, k * ATOMS : (k + 1) * ATOMS] = jnp.where(rows == slots[k : k + 1], 1.0, 0.0).astype(BF16)


def first_kernel(
    pack, from_a, from_b, hot, list_a, list_b, in_t, out_t, update_t,
    hidden, send_a, send_b, update_one, pairs, rows_one,
):
    _, _, domain = place()
    shift = jnp.where(domain == 0, -DOMAINS, jnp.where(domain == DOMAINS - 1, DOMAINS, 0)).astype(F32)
    own = coords_of(pack[0:HALO_ROWS, :])
    first = lax.broadcasted_iota(jnp.int32, (8, ATOMS), 0) == 0
    far = coords_of(from_b[...]) + jnp.where(first, shift, 0.0)
    far_rows = jnp.concatenate([p.astype(F32) for p in thirds(far)], axis=0).astype(BF16)
    ext_embed = jnp.concatenate([pack[0:CHANNELS, :], from_a[0:CHANNELS, :], from_b[0:CHANNELS, :]], axis=1)
    f32_rows = lambda ref: ref[ROW_POS:HALO_ROWS, :].astype(F32)
    far_full = jnp.concatenate([far_rows.astype(F32), jnp.zeros((8, ATOMS), F32)], axis=0)
    ext_pos = jnp.concatenate([f32_rows(pack), f32_rows(from_a), far_full], axis=1).astype(BF16)
    ext = jnp.concatenate([ext_embed, ext_pos], axis=0)
    own_wide = spread(own)
    centre = centres()
    message = jnp.zeros((CHANNELS, ATOMS), F32)
    for c in range(CHUNKS):
        got = dot(ext, hot[:, chunk(c)])
        vec = got[128:136] + got[136:144] + got[144:152] - own_wide
        pairs[:, chunk(c)] = vec
        sq = jnp.sum(vec * vec, axis=0, keepdims=True)
        scaled = (sq - centre) * (1.0 / BASIS_WIDTH)
        radial = jnp.exp(-scaled * scaled)
        pre = dot(in_t[0:128, 0 : 3 * BASIS], stacked(radial))
        act = (pre * gate(pre)).astype(BF16)
        filt = dot(out_t[0:128, :], act)
        rows = got[0:CHANNELS]
        rows_one[:, chunk(c)] = rows.astype(BF16)
        message = message + fold(filt * rows)
    upd = dot(update_t[0:128, :], message.astype(BF16))
    update_one[...] = upd
    hid = (pack[0:CHANNELS, :].astype(F32) + upd * gate(upd)).astype(BF16)
    hidden[...] = hid
    send_a[...] = dot(hid, list_a[...]).astype(BF16)
    send_b[...] = dot(hid, list_b[...]).astype(BF16)


def filters_kernel(pack, pairs, in_t, out_t, slope_one, slope_two, filter_two, own):
    own[...] = coords_of(pack[0:HALO_ROWS, :])
    centre = centres()
    for c in range(CHUNKS):
        vec = pairs[:, chunk(c)]
        sq = jnp.sum(vec * vec, axis=0, keepdims=True)
        scaled = (sq - centre) * (1.0 / BASIS_WIDTH)
        radial = jnp.exp(-scaled * scaled)
        tall = stacked(radial)
        steep = stacked(radial * scaled * (-2.0 / BASIS_WIDTH))
        for l, slope in ((0, slope_one), (1, slope_two)):
            weight = in_t[l * 128 : (l + 1) * 128, 0 : 3 * BASIS]
            pre = dot(weight, tall)
            change = dot(weight, steep)
            g = gate(pre)
            act = pre * g
            slope[:, chunk(c)] = ((g + act * (1.0 - g)) * change).astype(slope.dtype)
            if l == 1:
                filter_two[:, chunk(c)] = dot(out_t[128:256, :], act.astype(BF16))


def second_kernel(
    hidden, from_a, from_b, hot, filter_two, update_t, update, read,
    energy, grad_two, rows_two, grad_own, grad_a, grad_b,
):
    ext = jnp.concatenate([hidden[...], from_a[...], from_b[...]], axis=1)
    message = jnp.zeros((CHANNELS, ATOMS), F32)
    for c in range(CHUNKS):
        rows = dot(ext, hot[:, chunk(c)])
        rows_two[:, chunk(c)] = rows.astype(BF16)
        message = message + fold(filter_two[:, chunk(c)] * rows)
    upd = dot(update_t[128:256, :], message.astype(BF16))
    g = gate(upd)
    act = upd * g
    weight = read[...]
    energy[...] = jnp.broadcast_to(jnp.sum(act * weight, axis=0, keepdims=True), (8, ATOMS))
    dupd = ((g + act * (1.0 - g)) * weight).astype(BF16)
    grad = dot(update[1], dupd)
    grad_two[...] = grad
    wide = spread(grad)
    total = jnp.zeros((CHANNELS, EXT), F32)
    for c in range(CHUNKS):
        part = (filter_two[:, chunk(c)] * wide).astype(BF16)
        total = total + dot_nt(part, hot[:, chunk(c)])
    grad_own[...] = total[:, 0:ATOMS]
    grad_a[...] = total[:, ATOMS : 2 * ATOMS].astype(BF16)
    grad_b[...] = total[:, 2 * ATOMS :].astype(BF16)


def slope_kernel(grad_two, rows_two, slope_two, filter_out, out):
    wide = spread(grad_two[...])
    for c in range(CHUNKS):
        dfilt = (wide * rows_two[:, chunk(c)].astype(F32)).astype(BF16)
        dact = dot(filter_out[1], dfilt)
        part = jnp.sum(dact * slope_two[:, chunk(c)].astype(F32), axis=0, keepdims=True)
        out[:, chunk(c)] = jnp.broadcast_to(part, (8, CHUNK))


def third_kernel(
    grad_own, from_a, from_b, list_a, list_b, update_one, update, rows_one, slope_one,
    filter_out, dsq_two, pairs, hot,
    force, send_a, send_b,
):
    dhidden = grad_own[...] + dot_nt(from_a[...], list_a[...]) + dot_nt(from_b[...], list_b[...])
    upd = update_one[...]
    g = gate(upd)
    dupd = (dhidden * (g + upd * g * (1.0 - g))).astype(BF16)
    wide = spread(dot(update[0], dupd))
    own = jnp.zeros((8, ATOMS), F32)
    total = jnp.zeros((16, EXT), F32)
    for c in range(CHUNKS):
        dfilt = (wide * rows_one[:, chunk(c)].astype(F32)).astype(BF16)
        dact = dot(filter_out[0], dfilt)
        part = jnp.sum(dact * slope_one[:, chunk(c)].astype(F32), axis=0, keepdims=True)
        pull = 2.0 * (part + dsq_two[:, chunk(c)]) * pairs[:, chunk(c)]
        own = own + fold(pull)
        high, low = halves(pull)
        both = jnp.concatenate([high.astype(F32), low.astype(F32)], axis=0).astype(BF16)
        total = total + dot_nt(both, hot[:, chunk(c)])
    ext = total[0:8] + total[8:16]
    force[...] = own - ext[:, 0:ATOMS]
    send_a[...] = -ext[:, ATOMS : 2 * ATOMS]
    send_b[...] = -ext[:, 2 * ATOMS :]


def sums_kernel(force, from_a, from_b, list_a, list_b, own, prev, following, energy, pack, velocity, back, vec):
    image, _, _ = place()

    def returned(block, chosen):
        both = jnp.concatenate([p.astype(F32) for p in halves(block)], axis=0).astype(BF16)
        got = dot_nt(both, chosen)
        return got[0:8] + got[8:16]

    f = force[...] + returned(from_a[...], list_a[...]) + returned(from_b[...], list_b[...])
    ahead = following[...] - own[...]
    behind = own[...] - prev[...]
    back[0:8, :] = f
    back[8:16, :] = ahead
    back[16:24, :] = behind
    speed = velocity[0]
    movable = (image > 0) & (image < IMAGES - 1)
    down = lambda v: jnp.sum(v, axis=0, keepdims=True)
    level = pack[ROW_AUX : ROW_AUX + 8, :].astype(F32)[0:1] * (1.0 / ATOMS)
    rows = (
        energy[0:1, :],
        down(ahead * ahead),
        down(behind * behind),
        down(ahead * behind),
        down(f * ahead),
        down(f * behind),
        down(f * f),
        jnp.where(movable, down(speed * speed), 0.0),
        level,
    )
    lane = lax.broadcasted_iota(jnp.int32, (1, ATOMS), 1)
    total = jnp.zeros((1, ATOMS), F32)
    for j, row in enumerate(rows):
        total = jnp.where(lane == j, jnp.sum(row, axis=1, keepdims=True), total)
    vec[...] = jnp.broadcast_to(total, (DOMAINS, ATOMS))


def layer_kernel(parts, out):
    out[...] = jnp.broadcast_to(jnp.sum(parts[...], axis=0, keepdims=True), (IMAGES, ATOMS))


def final_kernel(table, back, pos, velocity, reset, spring, time_step, mixing, new_pos, new_speed, energy):
    image, _, _ = place()
    t = table[...]
    e, a, b, ab, fa, fb, ff, vv, level = (t[:, j : j + 1] for j in range(9))
    ahead_norm = jnp.sqrt(a + EPSILON)
    behind_norm = jnp.sqrt(b + EPSILON)
    tangent_sq = jnp.maximum(
        a / (ahead_norm * ahead_norm)
        + b / (behind_norm * behind_norm)
        + 2.0 * ab / (ahead_norm * behind_norm),
        0.0,
    )
    length = jnp.sqrt(tangent_sq + EPSILON)
    unit_sq = tangent_sq / (tangent_sq + EPSILON)
    parallel = (fa / ahead_norm + fb / behind_norm) / length
    tension = spring[0] * (ahead_norm - behind_norm)
    along = jnp.where(level > 0.5, -2.0 * parallel, tension - parallel)
    band_sq = ff + 2.0 * along * parallel + along * along * unit_sq
    row = lax.broadcasted_iota(jnp.int32, (IMAGES, 1), 0)
    inner = (row > 0) & (row < IMAGES - 1)
    down = lambda v: jnp.sum(v, axis=0, keepdims=True)
    force_norm = jnp.sqrt(down(jnp.where(inner, jnp.maximum(band_sq, 0.0), 0.0)) + EPSILON)
    speed_norm = jnp.sqrt(down(vv) + EPSILON)
    mine = row == image
    pick = lambda v: down(jnp.where(mine, v, 0.0))
    shape = (3, ATOMS)
    wide = lambda v: jnp.broadcast_to(jnp.broadcast_to(v, (1, ATOMS)), shape)
    energy[0] = jnp.sum(jnp.where(mine, e, 0.0))
    tangent = back[8:11, :] / wide(pick(ahead_norm)) + back[16:19, :] / wide(pick(behind_norm))
    band = back[0:3, :] + wide(pick(along / length)) * tangent
    speed = velocity[0]
    mix = mixing[0]
    mixed = (1.0 - mix) * speed + wide(mix * speed_norm / force_norm) * band
    kept = jnp.where(reset[0] > 0, 0.0, mixed)
    movable = (image > 0) & (image < IMAGES - 1)
    speed = jnp.where(movable, kept + time_step[0] * band, 0.0)
    new_speed[0] = speed
    new_pos[0] = pos[0] + time_step[0] * speed


VMEM = pl.BlockSpec(memory_space=pltpu.VMEM)
SMEM = pl.BlockSpec(memory_space=pltpu.SMEM)


def call(kernel, outs, args, scalars=(), scalar_outs=(), flops=0, limit=16 << 20):
    specs = [SMEM if i in scalars else VMEM for i in range(len(args))]
    moved = sum(a.size * a.dtype.itemsize for a in args)
    return pl.pallas_call(
        kernel,
        out_shape=[jax.ShapeDtypeStruct(s, t) for s, t in outs],
        in_specs=specs,
        out_specs=[SMEM if i in scalar_outs else VMEM for i in range(len(outs))],
        compiler_params=pltpu.CompilerParams(vmem_limit_bytes=limit),
        cost_estimate=pl.CostEstimate(flops=flops, bytes_accessed=moved, transcendentals=0),
        name=kernel.__name__,
    )(*args)


def per_device(
    positions, velocity, embed, neighbours, send_up, send_down, climb, reset,
    filter_in, filter_out, update_weight, readout, spring, time_step, mixing,
):
    square = (ATOMS, ATOMS)
    wide = (CHANNELS, PAIRS)
    (packed,) = call(
        pack_kernel,
        [((PACK_ROWS, ATOMS), BF16)],
        (positions, embed, neighbours, send_up.reshape(1, ATOMS), send_down.reshape(1, ATOMS), climb),
        scalars=(5,),
    )
    pack = move(packed, TO_WORKER)
    in_t, out_t, update_t, read = call(
        weights_kernel,
        [((256, 128), BF16), ((256, 128), BF16), ((256, 128), BF16), (square, F32)],
        (packed, filter_in, filter_out, update_weight, readout.reshape(1, CHANNELS)),
        flops=10**8,
    )
    list_a, list_b, send_a, send_b = call(
        lists_kernel,
        [(square, BF16), (square, BF16), ((HALO_ROWS, ATOMS), BF16), ((HALO_ROWS, ATOMS), BF16)],
        (pack,),
    )
    from_a, from_b = move(send_a, SWAP_A), move(send_b, SWAP_B)
    (hot,) = call(slots_kernel, [((EXT, PAIRS), BF16)], (pack,), flops=10**9)
    hidden, send_a, send_b, update_one, pairs, rows_one = call(
        first_kernel,
        [(square, BF16), (square, BF16), (square, BF16), (square, F32), ((8, PAIRS), F32), (wide, BF16)],
        (pack, from_a, from_b, hot, list_a, list_b, in_t, out_t, update_t),
        flops=10**9,
    )
    from_a, from_b = move(send_a, SWAP_A), move(send_b, SWAP_B)
    slope_one, slope_two, filter_two, own = call(
        filters_kernel,
        [(wide, BF16), (wide, BF16), (wide, F32), ((8, ATOMS), F32)],
        (pack, pairs, in_t, out_t),
        flops=10**9,
    )
    energy, grad_two, rows_two, grad_own, send_a, send_b = call(
        second_kernel,
        [((8, ATOMS), F32), (square, F32), (wide, BF16), (square, F32), (square, BF16), (square, BF16)],
        (hidden, from_a, from_b, hot, filter_two, update_t, update_weight, read),
        flops=10**9,
    )
    from_a, from_b = move(send_a, SWAP_A), move(send_b, SWAP_B)
    prev, following = move(own, IMAGE_UP), move(own, IMAGE_DOWN)
    (dsq_two,) = call(
        slope_kernel,
        [((8, PAIRS), F32)],
        (grad_two, rows_two, slope_two, filter_out),
        flops=10**9,
    )
    force, send_a, send_b = call(
        third_kernel,
        [((8, ATOMS), F32)] * 3,
        (
            grad_own, from_a, from_b, list_a, list_b, update_one, update_weight, rows_one,
            slope_one, filter_out, dsq_two, pairs, hot,
        ),
        flops=10**9,
    )
    from_a, from_b = move(send_a, SWAP_A), move(send_b, SWAP_B)
    back, vec = call(
        sums_kernel,
        [((24, ATOMS), F32), ((DOMAINS, ATOMS), F32)],
        (force, from_a, from_b, list_a, list_b, own, prev, following, energy, pack, velocity),
    )
    back = move(back, TO_HOME)
    parts = lax.all_to_all(vec, AXES, 0, 0, tiled=True, axis_index_groups=LAYERS)
    (layer,) = call(layer_kernel, [((IMAGES, ATOMS), F32)], (parts,))
    table = lax.all_to_all(layer, AXES, 0, 0, tiled=True, axis_index_groups=COLUMNS)
    new_pos, new_speed, energies = call(
        final_kernel,
        [((1, 3, ATOMS), F32), ((1, 3, ATOMS), F32), ((1,), F32)],
        (
            table, back, positions, velocity, reset,
            spring.reshape(1), time_step.reshape(1), mixing.reshape(1),
        ),
        scalars=(4, 5, 6, 7),
        scalar_outs=(2,),
    )
    return new_pos, new_speed, energies


def solution(mesh):
    placed = (
        P("image", None, "space"),
        P("image", None, "space"),
        P("space", None),
        P("space", None),
        P("space"),
        P("space"),
        P("image"),
        P("image"),
    ) + (P(),) * 7
    return jax.shard_map(
        per_device,
        mesh=mesh,
        in_specs=placed,
        out_specs=(P("image", None, "space"), P("image", None, "space"), P("image")),
        check_vma=False,
    )
```

```python
import jax
import jax.numpy as jnp
from jax import lax
from jax.experimental import pallas as pl
from jax.experimental.pallas import tpu as pltpu
from jax.sharding import PartitionSpec as P

EPSILON = 1e-06
BASIS_WIDTH = 0.6
BASIS_REACH = 6.0
BASIS = 16
IMAGES = 16
DOMAINS = 32
ATOMS = 128
CHANNELS = 128
SLOTS = 32
PAIRS = ATOMS * SLOTS
CHUNK = 512
PER_CHUNK = CHUNK // ATOMS
CHUNKS = PAIRS // CHUNK
EXT = 3 * ATOMS
AXES = ("image", "space")
F32 = jnp.float32
BF16 = jnp.bfloat16

ROW_POS = 128
ROW_AUX = 152
ROW_NEAR = 160
PACK_ROWS = 192
HALO_ROWS = 160
BLOCK = 5


def device_at(x, y, z, core):
    return ((y * 2 + z // 8) * 2 + core) * DOMAINS + x * 8 + z % 8


def home(image, domain):
    return image * DOMAINS + domain


def worker(image, domain):
    x, rest = divmod(domain, 8)
    pair, core = divmod(rest, 2)
    y, half, side = image // 4, image // 2 % 2, image % 2
    return device_at(x, pair if x % 2 else 3 - pair, half * 8 + y * 2 + side, core)


CELLS = [(i, d) for i in range(IMAGES) for d in range(DOMAINS)]
TO_WORKER = [(home(i, d), worker(i, d)) for i, d in CELLS]
SWAP_A = [(worker(i, d), worker(i, d ^ 1)) for i, d in CELLS]
SWAP_B = [(worker(i, d), worker(i, (d + 1) % DOMAINS if d % 2 else (d - 1) % DOMAINS)) for i, d in CELLS]
LAYERS = [[worker(i, d) for d in range(DOMAINS)] for i in range(IMAGES)]
COLUMNS = [[worker(i, d) for i in range(IMAGES)] for d in range(DOMAINS)]


def move(values, pairs):
    return lax.ppermute(values, AXES, pairs)


def place():
    image, space = lax.axis_index("image"), lax.axis_index("space")
    x, y = lax.shift_right_logical(space, 3), lax.shift_right_logical(image, 2)
    pair = jnp.where((x & 1) == 0, 3 - y, y)
    return image, lax.shift_right_logical(image, 1) & 1, x * 8 + pair * 2 + (image & 1)


def dot(a, b):
    return jnp.dot(a, b, preferred_element_type=F32)


def dot_nt(a, b):
    return lax.dot_general(a, b, (((1,), (1,)), ((), ())), preferred_element_type=F32)


def gate(v):
    return 0.5 * jnp.tanh(0.5 * v) + 0.5


def halves(v):
    high = v.astype(BF16)
    return high, (v - high.astype(F32)).astype(BF16)


def thirds(v):
    high = v.astype(BF16)
    rest = v - high.astype(F32)
    middle = rest.astype(BF16)
    return high, middle, (rest - middle.astype(F32)).astype(BF16)


def centres():
    step = BASIS_REACH / (BASIS - 1)
    return lax.broadcasted_iota(jnp.int32, (BASIS, CHUNK), 0).astype(F32) * step


def stacked(v):
    high, low = halves(v)
    return jnp.concatenate([high, low, high], axis=0)


def chunk(c):
    return pl.ds(c * CHUNK, CHUNK)


def fold(v):
    total = v[:, :ATOMS]
    for k in range(1, PER_CHUNK):
        total = total + v[:, k * ATOMS : (k + 1) * ATOMS]
    return total


def spread(v):
    return jnp.concatenate([v] * PER_CHUNK, axis=1)


def flat(ref):
    return jnp.concatenate([ref[0], ref[1], ref[2]], axis=0)


def coords_of(block):
    b = block[ROW_POS : ROW_POS + 24].astype(F32)
    return b[0:8] + b[8:16] + b[16:24]


def pack_kernel(
    pos_in, embed_in, near_in, up_in, down_in, out,
    pos, embed, near, up, down, sems,
):
    pairs = ((embed_in, embed), (near_in, near), (pos_in, pos), (up_in, up), (down_in, down))
    copies = [pltpu.make_async_copy(a, b, sems.at[i]) for i, (a, b) in enumerate(pairs)]
    for copy in copies:
        copy.start()
    copies[0].wait()
    out[0:CHANNELS, :] = embed[...].astype(F32).T.astype(BF16)
    copies[1].wait()
    out[ROW_NEAR:PACK_ROWS, :] = (near[...].astype(F32) - float(ATOMS)).astype(BF16)
    for copy in copies[2:]:
        copy.wait()
    zeros = jnp.zeros((5, ATOMS), F32)
    parts = [jnp.concatenate([p.astype(F32), zeros], axis=0) for p in thirds(flat(pos))]
    aux = jnp.concatenate([up[...].astype(F32), down[...].astype(F32), zeros, zeros[:1]], axis=0)
    out[ROW_POS:ROW_NEAR, :] = jnp.concatenate(parts + [aux], axis=0).astype(BF16)


def weights_kernel(
    after, filter_in, filter_out, update, readout, reset, spring, time_step, mixing,
    in_t, out_t, update_t, read, settings,
):
    for j, value in enumerate((reset[0].astype(F32), spring[0], time_step[0], mixing[0])):
        settings[j : j + 1, :] = jnp.full((1, ATOMS), value, F32)
    settings[4:8, :] = jnp.zeros((4, ATOMS), F32)
    for l in range(2):
        rows = pl.ds(l * 128, 128)
        high, low = halves(filter_in[l])
        filler = jnp.zeros((128 - 3 * BASIS, CHANNELS), F32)
        tall = jnp.concatenate(
            [high.astype(F32), high.astype(F32), low.astype(F32), filler], axis=0
        )
        in_t[rows, :] = tall.T.astype(BF16)
        out_t[rows, :] = filter_out[l].astype(F32).T.astype(BF16)
        update_t[rows, :] = update[l].astype(F32).T.astype(BF16)
    read[...] = jnp.broadcast_to(readout[...], (CHANNELS, ATOMS)).T


def lists_kernel(pack, list_a, list_b, send_a, send_b):
    _, _, domain = place()
    even = (domain & 1) == 0
    aux = pack[ROW_AUX : ROW_AUX + 8, :].astype(F32)
    up, down = aux[0:1], aux[1:2]
    rows = lax.broadcasted_iota(jnp.int32, (ATOMS, ATOMS), 0).astype(F32)
    block = pack[0:HALO_ROWS, :]
    for ids, chosen, send in (
        (jnp.where(even, up, down), list_a, send_a),
        (jnp.where(even, down, up), list_b, send_b),
    ):
        hot = jnp.where(rows == ids, 1.0, 0.0).astype(BF16)
        chosen[...] = hot
        send[...] = dot(block, hot).astype(BF16)


def slots_kernel(pack, hot, own):
    own[...] = coords_of(pack[0:HALO_ROWS, :])
    _, _, domain = place()
    even = (domain & 1) == 0
    slots = pack[ROW_NEAR:PACK_ROWS, :].astype(F32)
    swapped = jnp.where(slots < 0.0, slots, jnp.where(slots < 128.0, slots + 128.0, slots - 128.0))
    slots = jnp.where(even, swapped, slots)
    rows = lax.broadcasted_iota(jnp.int32, (EXT, ATOMS), 0).astype(F32) - float(ATOMS)
    for k in range(SLOTS):
        hot[:, k * ATOMS : (k + 1) * ATOMS] = jnp.where(rows == slots[k : k + 1], 1.0, 0.0).astype(BF16)


def first_kernel(
    pack, from_a, from_b, hot, list_a, list_b, in_t, out_t, update_t,
    hidden, send_a, send_b, update_one, pairs, rows_one,
):
    _, _, domain = place()
    shift = jnp.where(domain == 0, -DOMAINS, jnp.where(domain == DOMAINS - 1, DOMAINS, 0)).astype(F32)
    own = coords_of(pack[0:HALO_ROWS, :])
    first = lax.broadcasted_iota(jnp.int32, (8, ATOMS), 0) == 0
    far = coords_of(from_b[...]) + jnp.where(first, shift, 0.0)
    far_rows = jnp.concatenate([p.astype(F32) for p in thirds(far)], axis=0).astype(BF16)
    ext_embed = jnp.concatenate([pack[0:CHANNELS, :], from_a[0:CHANNELS, :], from_b[0:CHANNELS, :]], axis=1)
    f32_rows = lambda ref: ref[ROW_POS:HALO_ROWS, :].astype(F32)
    far_full = jnp.concatenate([far_rows.astype(F32), jnp.zeros((8, ATOMS), F32)], axis=0)
    ext_pos = jnp.concatenate([f32_rows(pack), f32_rows(from_a), far_full], axis=1).astype(BF16)
    ext = jnp.concatenate([ext_embed, ext_pos], axis=0)
    own_wide = spread(own)
    centre = centres()
    message = jnp.zeros((CHANNELS, ATOMS), F32)
    for c in range(CHUNKS):
        got = dot(ext, hot[:, chunk(c)])
        vec = got[128:136] + got[136:144] + got[144:152] - own_wide
        pairs[:, chunk(c)] = vec
        sq = jnp.sum(vec * vec, axis=0, keepdims=True)
        scaled = (sq - centre) * (1.0 / BASIS_WIDTH)
        radial = jnp.exp(-scaled * scaled)
        pre = dot(in_t[0:128, 0 : 3 * BASIS], stacked(radial))
        act = (pre * gate(pre)).astype(BF16)
        filt = dot(out_t[0:128, :], act)
        rows = got[0:CHANNELS]
        rows_one[:, chunk(c)] = rows.astype(BF16)
        message = message + fold(filt * rows)
    upd = dot(update_t[0:128, :], message.astype(BF16))
    update_one[...] = upd
    hid = (pack[0:CHANNELS, :].astype(F32) + upd * gate(upd)).astype(BF16)
    hidden[...] = hid
    send_a[...] = dot(hid, list_a[...]).astype(BF16)
    send_b[...] = dot(hid, list_b[...]).astype(BF16)


def filters_kernel(pairs, in_t, out_t, slope_one, slope_two, filter_two):
    centre = centres()
    for c in range(CHUNKS):
        vec = pairs[:, chunk(c)]
        sq = jnp.sum(vec * vec, axis=0, keepdims=True)
        scaled = (sq - centre) * (1.0 / BASIS_WIDTH)
        radial = jnp.exp(-scaled * scaled)
        tall = stacked(radial)
        steep = stacked(radial * scaled * (-2.0 / BASIS_WIDTH))
        for l, slope in ((0, slope_one), (1, slope_two)):
            weight = in_t[l * 128 : (l + 1) * 128, 0 : 3 * BASIS]
            pre = dot(weight, tall)
            change = dot(weight, steep)
            g = gate(pre)
            act = pre * g
            slope[:, chunk(c)] = ((g + act * (1.0 - g)) * change).astype(slope.dtype)
            if l == 1:
                filter_two[:, chunk(c)] = dot(out_t[128:256, :], act.astype(BF16))


def second_kernel(
    hidden, from_a, from_b, hot, filter_two, update_t, update, read,
    energy, grad_two, rows_two, grad_own, grad_a, grad_b,
):
    ext = jnp.concatenate([hidden[...], from_a[...], from_b[...]], axis=1)
    message = jnp.zeros((CHANNELS, ATOMS), F32)
    for c in range(CHUNKS):
        rows = dot(ext, hot[:, chunk(c)])
        rows_two[:, chunk(c)] = rows.astype(BF16)
        message = message + fold(filter_two[:, chunk(c)] * rows)
    upd = dot(update_t[128:256, :], message.astype(BF16))
    g = gate(upd)
    act = upd * g
    weight = read[...]
    energy[...] = jnp.broadcast_to(jnp.sum(act * weight, axis=0, keepdims=True), (8, ATOMS))
    dupd = ((g + act * (1.0 - g)) * weight).astype(BF16)
    grad = dot(update[1], dupd)
    grad_two[...] = grad
    wide = spread(grad)
    total = jnp.zeros((CHANNELS, EXT), F32)
    for c in range(CHUNKS):
        part = (filter_two[:, chunk(c)] * wide).astype(BF16)
        total = total + dot_nt(part, hot[:, chunk(c)])
    grad_own[...] = total[:, 0:ATOMS]
    grad_a[...] = total[:, ATOMS : 2 * ATOMS].astype(BF16)
    grad_b[...] = total[:, 2 * ATOMS :].astype(BF16)


def slope_kernel(grad_two, rows_two, slope_two, filter_out, out):
    wide = spread(grad_two[...])
    for c in range(CHUNKS):
        dfilt = (wide * rows_two[:, chunk(c)].astype(F32)).astype(BF16)
        dact = dot(filter_out[1], dfilt)
        part = jnp.sum(dact * slope_two[:, chunk(c)].astype(F32), axis=0, keepdims=True)
        out[:, chunk(c)] = jnp.broadcast_to(part, (8, CHUNK))


def third_kernel(
    grad_own, from_a, from_b, list_a, list_b, update_one, update, rows_one, slope_one,
    filter_out, dsq_two, pairs, hot,
    force, send_a, send_b,
):
    dhidden = grad_own[...] + dot_nt(from_a[...], list_a[...]) + dot_nt(from_b[...], list_b[...])
    upd = update_one[...]
    g = gate(upd)
    dupd = (dhidden * (g + upd * g * (1.0 - g))).astype(BF16)
    wide = spread(dot(update[0], dupd))
    own = jnp.zeros((8, ATOMS), F32)
    total = jnp.zeros((16, EXT), F32)
    for c in range(CHUNKS):
        dfilt = (wide * rows_one[:, chunk(c)].astype(F32)).astype(BF16)
        dact = dot(filter_out[0], dfilt)
        part = jnp.sum(dact * slope_one[:, chunk(c)].astype(F32), axis=0, keepdims=True)
        pull = 2.0 * (part + dsq_two[:, chunk(c)]) * pairs[:, chunk(c)]
        own = own + fold(pull)
        high, low = halves(pull)
        both = jnp.concatenate([high.astype(F32), low.astype(F32)], axis=0).astype(BF16)
        total = total + dot_nt(both, hot[:, chunk(c)])
    ext = total[0:8] + total[8:16]
    force[...] = own - ext[:, 0:ATOMS]
    send_a[...] = -ext[:, ATOMS : 2 * ATOMS]
    send_b[...] = -ext[:, 2 * ATOMS :]


def sums_kernel(force, from_a, from_b, list_a, list_b, own, energy, velocity, climb, out):
    image, _, _ = place()

    def returned(block, chosen):
        both = jnp.concatenate([p.astype(F32) for p in halves(block)], axis=0).astype(BF16)
        got = dot_nt(both, chosen)
        return got[0:8] + got[8:16]

    f = force[...] + returned(from_a[...], list_a[...]) + returned(from_b[...], list_b[...])
    speed = flat(velocity)
    movable = (image > 0) & (image < IMAGES - 1)
    speed_sq = jnp.where(movable, jnp.sum(speed * speed), 0.0)
    lane = lax.broadcasted_iota(jnp.int32, (1, ATOMS), 1)
    last = jnp.where(lane == 6 * IMAGES, speed_sq, 0.0)
    last = jnp.where(lane == 7 * IMAGES + image, climb[0].astype(F32), last)
    block = jnp.concatenate([f[0:3], own[0:3, :], energy[0:1, :], last], axis=0)
    for j in range(IMAGES):
        out[j * 8 : (j + 1) * 8, :] = block


def column_kernel(blocks, out):
    _, half, _ = place()
    part = lambda r: blocks[pl.ds(r, IMAGES, stride=8), :]
    force = [part(r) for r in range(3)]
    coords = [part(r + 3) for r in range(3)]
    ahead = [jnp.concatenate([p[1:], p[-1:]], axis=0) - p for p in coords]
    behind = [p - jnp.concatenate([p[:1], p[:-1]], axis=0) for p in coords]
    inner = lambda u, v: u[0] * v[0] + u[1] * v[1] + u[2] * v[2]
    rows = [
        part(6),
        inner(ahead, ahead),
        inner(ahead, behind),
        inner(force, ahead),
        inner(force, behind),
        inner(force, force),
        jnp.zeros((2 * IMAGES, ATOMS), F32),
    ]
    square = jnp.concatenate(rows, axis=0)
    table = jnp.sum(square.T, axis=0, keepdims=True) + jnp.sum(part(7), axis=0, keepdims=True)
    parts = force + ahead + behind
    for y in range(4):
        for core in range(2):
            low = y * 4 + core
            pick = lambda v: jnp.where(half == 0, v[low : low + 1], v[low + 2 : low + 3])
            lines = [table] + [pick(v) for v in parts]
            pairs = [jnp.concatenate(lines[2 * r : 2 * r + 2], axis=0) for r in range(BLOCK)]
            for x in range(4):
                target = x * 8 + (y if x % 2 else 3 - y) * 2 + core
                for r in range(BLOCK):
                    out[target * BLOCK + r] = pairs[r]


def final_kernel(blocks, pos, velocity, settings, new_pos, new_speed, energy):
    image, _, _ = place()
    space = lax.axis_index("space")
    reset, spring, step, mix = (settings[j : j + 1, :] for j in range(4))
    total = blocks[0]
    for j in range(1, DOMAINS):
        total = total + blocks[j * BLOCK]
    row = lax.broadcasted_iota(jnp.int32, (IMAGES, 1), 0)
    lane = lax.broadcasted_iota(jnp.int32, (IMAGES, ATOMS), 1)
    table = jnp.broadcast_to(total[0:1], (IMAGES, ATOMS))
    column = lambda j: jnp.sum(jnp.where(lane == row + j * IMAGES, table, 0.0), axis=1, keepdims=True)
    e, a, ab, fa, fb, ff, vv, level = (column(j) for j in range(8))
    b = jnp.concatenate([a[:1], a[:-1]], axis=0)
    down = lambda v: jnp.sum(v, axis=0, keepdims=True)
    ahead_norm = jnp.sqrt(a + EPSILON)
    behind_norm = jnp.sqrt(b + EPSILON)
    tangent_sq = jnp.maximum(
        a / (ahead_norm * ahead_norm)
        + b / (behind_norm * behind_norm)
        + 2.0 * ab / (ahead_norm * behind_norm),
        0.0,
    )
    length = jnp.sqrt(tangent_sq + EPSILON)
    unit_sq = tangent_sq / (tangent_sq + EPSILON)
    parallel = (fa / ahead_norm + fb / behind_norm) / length
    tension = spring[:, 0:1] * (ahead_norm - behind_norm)
    along = jnp.where(level > 0.5, -2.0 * parallel, tension - parallel)
    band_sq = ff + 2.0 * along * parallel + along * along * unit_sq
    inner = (row > 0) & (row < IMAGES - 1)
    force_norm = jnp.sqrt(down(jnp.where(inner, jnp.maximum(band_sq, 0.0), 0.0)) + EPSILON)
    speed_norm = jnp.sqrt(down(vv) + EPSILON)
    mine = row == image
    pick = lambda v: down(jnp.where(mine, v, 0.0))
    wide = lambda v: jnp.broadcast_to(jnp.broadcast_to(v, (1, ATOMS)), (3, ATOMS))
    energy[0] = jnp.sum(jnp.where(mine, e, 0.0))
    back = jnp.concatenate([blocks[space * BLOCK + r] for r in range(BLOCK)], axis=0)
    tangent = back[4:7] / wide(pick(ahead_norm)) + back[7:10] / wide(pick(behind_norm))
    band = back[1:4] + wide(pick(along / length)) * tangent
    speed = flat(velocity)
    mixed = wide(1.0 - mix) * speed + wide(mix * speed_norm / force_norm) * band
    kept = jnp.where(wide(reset) > 0.5, 0.0, mixed)
    movable = (image > 0) & (image < IMAGES - 1)
    speed = jnp.where(movable, kept + wide(step) * band, 0.0)
    moved = flat(pos) + wide(step) * speed
    for j in range(3):
        new_speed[j] = speed[j : j + 1]
        new_pos[j] = moved[j : j + 1]


VMEM = pl.BlockSpec(memory_space=pltpu.VMEM)
SMEM = pl.BlockSpec(memory_space=pltpu.SMEM)


def call(kernel, outs, args, scalars=(), scalar_outs=(), flops=0, limit=16 << 20):
    specs = [SMEM if i in scalars else VMEM for i in range(len(args))]
    moved = sum(a.size * a.dtype.itemsize for a in args)
    return pl.pallas_call(
        kernel,
        out_shape=[jax.ShapeDtypeStruct(s, t) for s, t in outs],
        in_specs=specs,
        out_specs=[SMEM if i in scalar_outs else VMEM for i in range(len(outs))],
        compiler_params=pltpu.CompilerParams(vmem_limit_bytes=limit),
        cost_estimate=pl.CostEstimate(flops=flops, bytes_accessed=moved, transcendentals=0),
        name=kernel.__name__,
    )(*args)


def pack_call(*args):
    return pl.pallas_call(
        pack_kernel,
        out_shape=jax.ShapeDtypeStruct((PACK_ROWS, ATOMS), BF16),
        in_specs=[pl.BlockSpec(memory_space=pltpu.HBM)] * len(args),
        out_specs=VMEM,
        scratch_shapes=[pltpu.VMEM(a.shape, a.dtype) for a in args]
        + [pltpu.SemaphoreType.DMA((len(args),))],
        compiler_params=pltpu.CompilerParams(vmem_limit_bytes=60 << 20),
        name="pack_kernel",
    )(*args)


def per_device(
    positions, velocity, embed, neighbours, send_up, send_down, climb, reset,
    filter_in, filter_out, update_weight, readout, spring, time_step, mixing,
):
    square = (ATOMS, ATOMS)
    wide = (CHANNELS, PAIRS)
    positions = positions.transpose(1, 0, 2)
    velocity = velocity.transpose(1, 0, 2)
    packed = pack_call(
        positions, embed, neighbours.T, send_up.reshape(1, ATOMS), send_down.reshape(1, ATOMS)
    )
    pack = move(packed, TO_WORKER)
    in_t, out_t, update_t, read, settings = call(
        weights_kernel,
        [((256, 128), BF16), ((256, 128), BF16), ((256, 128), BF16), (square, F32), ((8, ATOMS), F32)],
        (
            packed, filter_in, filter_out, update_weight, readout.reshape(1, CHANNELS),
            reset, spring.reshape(1), time_step.reshape(1), mixing.reshape(1),
        ),
        scalars=(5, 6, 7, 8),
        flops=10**8,
        limit=60 << 20,
    )
    list_a, list_b, send_a, send_b = call(
        lists_kernel,
        [(square, BF16), (square, BF16), ((HALO_ROWS, ATOMS), BF16), ((HALO_ROWS, ATOMS), BF16)],
        (pack,),
    )
    from_a, from_b = move(send_a, SWAP_A), move(send_b, SWAP_B)
    hot, own = call(slots_kernel, [((EXT, PAIRS), BF16), ((8, ATOMS), F32)], (pack,), flops=10**9)
    hidden, send_a, send_b, update_one, pairs, rows_one = call(
        first_kernel,
        [(square, BF16), (square, BF16), (square, BF16), (square, F32), ((8, PAIRS), F32), (wide, BF16)],
        (pack, from_a, from_b, hot, list_a, list_b, in_t, out_t, update_t),
        flops=10**9,
    )
    from_a, from_b = move(send_a, SWAP_A), move(send_b, SWAP_B)
    slope_one, slope_two, filter_two = call(
        filters_kernel,
        [(wide, BF16), (wide, BF16), (wide, F32)],
        (pairs, in_t, out_t),
        flops=10**9,
    )
    energy, grad_two, rows_two, grad_own, send_a, send_b = call(
        second_kernel,
        [((8, ATOMS), F32), (square, F32), (wide, BF16), (square, F32), (square, BF16), (square, BF16)],
        (hidden, from_a, from_b, hot, filter_two, update_t, update_weight, read),
        flops=10**9,
    )
    from_a, from_b = move(send_a, SWAP_A), move(send_b, SWAP_B)
    (dsq_two,) = call(
        slope_kernel,
        [((8, PAIRS), F32)],
        (grad_two, rows_two, slope_two, filter_out),
        flops=10**9,
    )
    force, send_a, send_b = call(
        third_kernel,
        [((8, ATOMS), F32)] * 3,
        (
            grad_own, from_a, from_b, list_a, list_b, update_one, update_weight, rows_one,
            slope_one, filter_out, dsq_two, pairs, hot,
        ),
        flops=10**9,
    )
    from_a, from_b = move(send_a, SWAP_A), move(send_b, SWAP_B)
    (blocks,) = call(
        sums_kernel,
        [((IMAGES * 8, ATOMS), F32)],
        (force, from_a, from_b, list_a, list_b, own, energy, velocity, climb),
        scalars=(8,),
    )
    column = lax.all_to_all(blocks, AXES, 0, 0, tiled=True, axis_index_groups=COLUMNS)
    (blocks,) = call(column_kernel, [((DOMAINS * BLOCK, 2, ATOMS), F32)], (column,))
    table = lax.all_to_all(blocks, AXES, 0, 0, tiled=True, axis_index_groups=LAYERS)
    new_pos, new_speed, energies = call(
        final_kernel,
        [((3, 1, ATOMS), F32), ((3, 1, ATOMS), F32), ((1,), F32)],
        (table, positions, velocity, settings),
        scalar_outs=(2,),
    )
    return new_pos.transpose(1, 0, 2), new_speed.transpose(1, 0, 2), energies


def solution(mesh):
    placed = (
        P("image", None, "space"),
        P("image", None, "space"),
        P("space", None),
        P("space", None),
        P("space"),
        P("space"),
        P("image"),
        P("image"),
    ) + (P(),) * 7
    return jax.shard_map(
        per_device,
        mesh=mesh,
        in_specs=placed,
        out_specs=(P("image", None, "space"), P("image", None, "space"), P("image")),
        check_vma=False,
    )
```

```python
import jax
import jax.numpy as jnp
from jax import lax
from jax.experimental import pallas as pl
from jax.experimental.pallas import tpu as pltpu
from jax.sharding import PartitionSpec as P

EPSILON = 1e-06
BASIS_WIDTH = 0.6
BASIS_REACH = 6.0
BASIS = 16
IMAGES = 16
DOMAINS = 32
ATOMS = 128
CHANNELS = 128
SLOTS = 32
PAIRS = ATOMS * SLOTS
CHUNK = 2048
PER_CHUNK = CHUNK // ATOMS
CHUNKS = PAIRS // CHUNK
EXT = 3 * ATOMS
AXES = ("image", "space")
F32 = jnp.float32
BF16 = jnp.bfloat16

ROW_POS = 128
ROW_AUX = 152
ROW_NEAR = 160
PACK_ROWS = 192
HALO_ROWS = 160
BLOCK = 5


def device_at(x, y, z, core):
    return ((y * 2 + z // 8) * 2 + core) * DOMAINS + x * 8 + z % 8


def home(image, domain):
    return image * DOMAINS + domain


RING = [
    (1, 2), (1, 3), (0, 3), (0, 2), (0, 1), (0, 0), (1, 0), (1, 1),
    (2, 1), (2, 0), (3, 0), (3, 1), (3, 2), (3, 3), (2, 3), (2, 2),
]
LAYER_PAIR = (1, 0, 3, 2)


def worker(image, domain):
    x, y = RING[domain // 2]
    home_y, half, side = image // 4, image // 2 % 2, image % 2
    return device_at(x, y, half * 8 + LAYER_PAIR[home_y] * 2 + side, domain % 2)


CELLS = [(i, d) for i in range(IMAGES) for d in range(DOMAINS)]
TO_WORKER = [(home(i, d), worker(i, d)) for i, d in CELLS]
SWAP_A = [(worker(i, d), worker(i, d ^ 1)) for i, d in CELLS]
SWAP_B = [(worker(i, d), worker(i, (d + 1) % DOMAINS if d % 2 else (d - 1) % DOMAINS)) for i, d in CELLS]
LAYERS = [[worker(i, d) for d in range(DOMAINS)] for i in range(IMAGES)]
COLUMNS = [[worker(i, d) for i in range(IMAGES)] for d in range(DOMAINS)]


def move(values, pairs):
    return lax.ppermute(values, AXES, pairs)


def place():
    image, space = lax.axis_index("image"), lax.axis_index("space")
    cell = (lax.shift_right_logical(space, 3) << 2) + lax.shift_right_logical(image, 2)
    pair = jnp.int32(0)
    for step, (x, y) in enumerate(RING):
        pair = jnp.where(cell == x * 4 + y, step, pair)
    return image, lax.shift_right_logical(image, 1) & 1, pair * 2 + (image & 1)


def dot(a, b):
    return jnp.dot(a, b, preferred_element_type=F32)


def dot_nt(a, b):
    return lax.dot_general(a, b, (((1,), (1,)), ((), ())), preferred_element_type=F32)


def gate(v):
    return 0.5 * jnp.tanh(0.5 * v) + 0.5


def halves(v):
    high = v.astype(BF16)
    return high, (v - high.astype(F32)).astype(BF16)


def thirds(v):
    high = v.astype(BF16)
    rest = v - high.astype(F32)
    middle = rest.astype(BF16)
    return high, middle, (rest - middle.astype(F32)).astype(BF16)


def centres():
    step = BASIS_REACH / (BASIS - 1)
    return lax.broadcasted_iota(jnp.int32, (BASIS, CHUNK), 0).astype(F32) * step


def stacked(v):
    high, low = halves(v)
    return jnp.concatenate([high, low, high], axis=0)


def chunk(c):
    return pl.ds(c * CHUNK, CHUNK)


def fold(v):
    total = v[:, :ATOMS]
    for k in range(1, PER_CHUNK):
        total = total + v[:, k * ATOMS : (k + 1) * ATOMS]
    return total


def spread(v):
    return jnp.concatenate([v] * PER_CHUNK, axis=1)


def flat(ref):
    return jnp.concatenate([ref[0], ref[1], ref[2]], axis=0)


def coords_of(block):
    b = block[ROW_POS : ROW_POS + 24].astype(F32)
    return b[0:8] + b[8:16] + b[16:24]


def pack_kernel(
    pos_in, embed_in, near_in, up_in, down_in, out,
    pos, embed, near, up, down, sems,
):
    pairs = ((embed_in, embed), (near_in, near), (pos_in, pos), (up_in, up), (down_in, down))
    copies = [pltpu.make_async_copy(a, b, sems.at[i]) for i, (a, b) in enumerate(pairs)]
    for copy in copies:
        copy.start()
    copies[0].wait()
    out[0:CHANNELS, :] = embed[...].astype(F32).T.astype(BF16)
    copies[1].wait()
    out[ROW_NEAR:PACK_ROWS, :] = (near[...].astype(F32) - float(ATOMS)).astype(BF16)
    for copy in copies[2:]:
        copy.wait()
    zeros = jnp.zeros((5, ATOMS), F32)
    parts = [jnp.concatenate([p.astype(F32), zeros], axis=0) for p in thirds(flat(pos))]
    aux = jnp.concatenate([up[...].astype(F32), down[...].astype(F32), zeros, zeros[:1]], axis=0)
    out[ROW_POS:ROW_NEAR, :] = jnp.concatenate(parts + [aux], axis=0).astype(BF16)


def weights_kernel(
    after, filter_in, filter_out, update, readout, reset, spring, time_step, mixing,
    in_t, out_t, update_t, read, settings,
):
    for j, value in enumerate((reset[0].astype(F32), spring[0], time_step[0], mixing[0])):
        settings[j : j + 1, :] = jnp.full((1, ATOMS), value, F32)
    settings[4:8, :] = jnp.zeros((4, ATOMS), F32)
    for l in range(2):
        rows = pl.ds(l * 128, 128)
        high, low = halves(0.5 * filter_in[l])
        filler = jnp.zeros((128 - 3 * BASIS, CHANNELS), F32)
        tall = jnp.concatenate(
            [high.astype(F32), high.astype(F32), low.astype(F32), filler], axis=0
        )
        in_t[rows, :] = tall.T.astype(BF16)
        out_t[rows, :] = filter_out[l].astype(F32).T.astype(BF16)
        update_t[rows, :] = update[l].astype(F32).T.astype(BF16)
    read[...] = jnp.broadcast_to(readout[...], (CHANNELS, ATOMS)).T


def lists_kernel(pack, list_a, list_b, send_a, send_b):
    _, _, domain = place()
    even = (domain & 1) == 0
    aux = pack[ROW_AUX : ROW_AUX + 8, :].astype(F32)
    up, down = aux[0:1], aux[1:2]
    rows = lax.broadcasted_iota(jnp.int32, (ATOMS, ATOMS), 0).astype(F32)
    block = pack[0:HALO_ROWS, :]
    for ids, chosen, send in (
        (jnp.where(even, up, down), list_a, send_a),
        (jnp.where(even, down, up), list_b, send_b),
    ):
        hot = jnp.where(rows == ids, 1.0, 0.0).astype(BF16)
        chosen[...] = hot
        send[...] = dot(block, hot).astype(BF16)


def slots_kernel(pack, hot, own):
    own[...] = coords_of(pack[0:HALO_ROWS, :])
    _, _, domain = place()
    even = (domain & 1) == 0
    slots = pack[ROW_NEAR:PACK_ROWS, :].astype(F32)
    swapped = jnp.where(slots < 0.0, slots, jnp.where(slots < 128.0, slots + 128.0, slots - 128.0))
    slots = jnp.where(even, swapped, slots)
    rows = lax.broadcasted_iota(jnp.int32, (EXT, ATOMS), 0).astype(F32) - float(ATOMS)
    for k in range(SLOTS):
        hot[:, k * ATOMS : (k + 1) * ATOMS] = jnp.where(rows == slots[k : k + 1], 1.0, 0.0).astype(BF16)


def first_kernel(
    pack, from_a, from_b, hot, list_a, list_b, in_t, out_t, update_t,
    hidden, send_a, send_b, update_one, pairs, rows_one,
):
    _, _, domain = place()
    shift = jnp.where(domain == 0, -DOMAINS, jnp.where(domain == DOMAINS - 1, DOMAINS, 0)).astype(F32)
    own = coords_of(pack[0:HALO_ROWS, :])
    first = lax.broadcasted_iota(jnp.int32, (8, ATOMS), 0) == 0
    far = coords_of(from_b[...]) + jnp.where(first, shift, 0.0)
    far_rows = jnp.concatenate([p.astype(F32) for p in thirds(far)], axis=0).astype(BF16)
    ext_embed = jnp.concatenate([pack[0:CHANNELS, :], from_a[0:CHANNELS, :], from_b[0:CHANNELS, :]], axis=1)
    f32_rows = lambda ref: ref[ROW_POS:HALO_ROWS, :].astype(F32)
    far_full = jnp.concatenate([far_rows.astype(F32), jnp.zeros((8, ATOMS), F32)], axis=0)
    ext_pos = jnp.concatenate([f32_rows(pack), f32_rows(from_a), far_full], axis=1).astype(BF16)
    ext = jnp.concatenate([ext_embed, ext_pos], axis=0)
    own_wide = spread(own)
    centre = centres()
    message = jnp.zeros((CHANNELS, ATOMS), F32)
    for c in range(CHUNKS):
        got = dot(ext, hot[:, chunk(c)])
        vec = got[128:136] + got[136:144] + got[144:152] - own_wide
        pairs[:, chunk(c)] = vec
        sq = jnp.sum(vec * vec, axis=0, keepdims=True)
        scaled = (sq - centre) * (1.0 / BASIS_WIDTH)
        radial = jnp.exp(-scaled * scaled)
        half = dot(in_t[0:128, 0 : 3 * BASIS], stacked(radial))
        act = (half + half * jnp.tanh(half)).astype(BF16)
        filt = dot(out_t[0:128, :], act)
        rows = got[0:CHANNELS]
        rows_one[:, chunk(c)] = rows.astype(BF16)
        message = message + fold(filt * rows)
    upd = dot(update_t[0:128, :], message.astype(BF16))
    update_one[...] = upd
    hid = (pack[0:CHANNELS, :].astype(F32) + upd * gate(upd)).astype(BF16)
    hidden[...] = hid
    send_a[...] = dot(hid, list_a[...]).astype(BF16)
    send_b[...] = dot(hid, list_b[...]).astype(BF16)


def filters_kernel(pairs, in_t, out_t, slope_one, slope_two, filter_two):
    centre = centres()
    for c in range(CHUNKS):
        vec = pairs[:, chunk(c)]
        sq = jnp.sum(vec * vec, axis=0, keepdims=True)
        scaled = (sq - centre) * (1.0 / BASIS_WIDTH)
        radial = jnp.exp(-scaled * scaled)
        tall = stacked(radial)
        steep = stacked(radial * scaled * (-2.0 / BASIS_WIDTH))
        for l, slope in ((0, slope_one), (1, slope_two)):
            weight = in_t[l * 128 : (l + 1) * 128, 0 : 3 * BASIS]
            half = dot(weight, tall)
            change = dot(weight, steep)
            t = jnp.tanh(half)
            bent = half * t
            slope[:, chunk(c)] = ((1.0 + t) * (1.0 + half - bent) * change).astype(slope.dtype)
            if l == 1:
                filter_two[:, chunk(c)] = dot(out_t[128:256, :], (half + bent).astype(BF16))


def second_kernel(
    hidden, from_a, from_b, hot, filter_two, update_t, update, read,
    energy, grad_two, rows_two, grad_own, grad_a, grad_b,
):
    ext = jnp.concatenate([hidden[...], from_a[...], from_b[...]], axis=1)
    message = jnp.zeros((CHANNELS, ATOMS), F32)
    for c in range(CHUNKS):
        rows = dot(ext, hot[:, chunk(c)])
        rows_two[:, chunk(c)] = rows.astype(BF16)
        message = message + fold(filter_two[:, chunk(c)] * rows)
    upd = dot(update_t[128:256, :], message.astype(BF16))
    g = gate(upd)
    act = upd * g
    weight = read[...]
    energy[...] = jnp.broadcast_to(jnp.sum(act * weight, axis=0, keepdims=True), (8, ATOMS))
    dupd = ((g + act * (1.0 - g)) * weight).astype(BF16)
    grad = dot(update[1], dupd)
    grad_two[...] = grad
    wide = spread(grad)
    total = jnp.zeros((CHANNELS, EXT), F32)
    for c in range(CHUNKS):
        part = (filter_two[:, chunk(c)] * wide).astype(BF16)
        total = total + dot_nt(part, hot[:, chunk(c)])
    grad_own[...] = total[:, 0:ATOMS]
    grad_a[...] = total[:, ATOMS : 2 * ATOMS].astype(BF16)
    grad_b[...] = total[:, 2 * ATOMS :].astype(BF16)


def slope_kernel(grad_two, rows_two, slope_two, filter_out, out):
    wide = spread(grad_two[...])
    for c in range(CHUNKS):
        dfilt = (wide * rows_two[:, chunk(c)].astype(F32)).astype(BF16)
        dact = dot(filter_out[1], dfilt)
        part = jnp.sum(dact * slope_two[:, chunk(c)].astype(F32), axis=0, keepdims=True)
        out[:, chunk(c)] = jnp.broadcast_to(part, (8, CHUNK))


def third_kernel(
    grad_own, from_a, from_b, list_a, list_b, update_one, update, rows_one, slope_one,
    filter_out, dsq_two, pairs, hot,
    force, send_a, send_b,
):
    dhidden = grad_own[...] + dot_nt(from_a[...], list_a[...]) + dot_nt(from_b[...], list_b[...])
    upd = update_one[...]
    g = gate(upd)
    dupd = (dhidden * (g + upd * g * (1.0 - g))).astype(BF16)
    wide = spread(dot(update[0], dupd))
    own = jnp.zeros((8, ATOMS), F32)
    total = jnp.zeros((16, EXT), F32)
    for c in range(CHUNKS):
        dfilt = (wide * rows_one[:, chunk(c)].astype(F32)).astype(BF16)
        dact = dot(filter_out[0], dfilt)
        part = jnp.sum(dact * slope_one[:, chunk(c)].astype(F32), axis=0, keepdims=True)
        pull = 2.0 * (part + dsq_two[:, chunk(c)]) * pairs[:, chunk(c)]
        own = own + fold(pull)
        high, low = halves(pull)
        both = jnp.concatenate([high.astype(F32), low.astype(F32)], axis=0).astype(BF16)
        total = total + dot_nt(both, hot[:, chunk(c)])
    ext = total[0:8] + total[8:16]
    force[...] = own - ext[:, 0:ATOMS]
    send_a[...] = -ext[:, ATOMS : 2 * ATOMS]
    send_b[...] = -ext[:, 2 * ATOMS :]


def sums_kernel(force, from_a, from_b, list_a, list_b, own, energy, velocity, climb, out):
    image, _, _ = place()

    def returned(block, chosen):
        both = jnp.concatenate([p.astype(F32) for p in halves(block)], axis=0).astype(BF16)
        got = dot_nt(both, chosen)
        return got[0:8] + got[8:16]

    f = force[...] + returned(from_a[...], list_a[...]) + returned(from_b[...], list_b[...])
    speed = flat(velocity)
    movable = (image > 0) & (image < IMAGES - 1)
    speed_sq = jnp.where(movable, jnp.sum(speed * speed), 0.0)
    lane = lax.broadcasted_iota(jnp.int32, (1, ATOMS), 1)
    last = jnp.where(lane == 6 * IMAGES, speed_sq, 0.0)
    last = jnp.where(lane == 7 * IMAGES + image, climb[0].astype(F32), last)
    block = jnp.concatenate([f[0:3], own[0:3, :], energy[0:1, :], last], axis=0)
    for j in range(IMAGES):
        out[j * 8 : (j + 1) * 8, :] = block


def column_kernel(blocks, out):
    _, half, _ = place()
    part = lambda r: blocks[pl.ds(r, IMAGES, stride=8), :]
    force = [part(r) for r in range(3)]
    coords = [part(r + 3) for r in range(3)]
    ahead = [jnp.concatenate([p[1:], p[-1:]], axis=0) - p for p in coords]
    behind = [p - jnp.concatenate([p[:1], p[:-1]], axis=0) for p in coords]
    inner = lambda u, v: u[0] * v[0] + u[1] * v[1] + u[2] * v[2]
    rows = [
        part(6),
        inner(ahead, ahead),
        inner(ahead, behind),
        inner(force, ahead),
        inner(force, behind),
        inner(force, force),
        jnp.zeros((2 * IMAGES, ATOMS), F32),
    ]
    square = jnp.concatenate(rows, axis=0)
    table = jnp.sum(square.T, axis=0, keepdims=True) + jnp.sum(part(7), axis=0, keepdims=True)
    parts = force + ahead + behind
    for y in range(4):
        for core in range(2):
            low = y * 4 + core
            pick = lambda v: jnp.where(half == 0, v[low : low + 1], v[low + 2 : low + 3])
            lines = [table] + [pick(v) for v in parts]
            pairs = [jnp.concatenate(lines[2 * r : 2 * r + 2], axis=0) for r in range(BLOCK)]
            for x in range(4):
                target = RING.index((x, y)) * 2 + core
                for r in range(BLOCK):
                    out[target * BLOCK + r] = pairs[r]


def final_kernel(blocks, pos, velocity, settings, new_pos, new_speed, energy):
    image, _, _ = place()
    space = lax.axis_index("space")
    reset, spring, step, mix = (settings[j : j + 1, :] for j in range(4))
    total = blocks[0]
    for j in range(1, DOMAINS):
        total = total + blocks[j * BLOCK]
    row = lax.broadcasted_iota(jnp.int32, (IMAGES, 1), 0)
    lane = lax.broadcasted_iota(jnp.int32, (IMAGES, ATOMS), 1)
    table = jnp.broadcast_to(total[0:1], (IMAGES, ATOMS))
    column = lambda j: jnp.sum(jnp.where(lane == row + j * IMAGES, table, 0.0), axis=1, keepdims=True)
    e, a, ab, fa, fb, ff, vv, level = (column(j) for j in range(8))
    b = jnp.concatenate([a[:1], a[:-1]], axis=0)
    down = lambda v: jnp.sum(v, axis=0, keepdims=True)
    ahead_norm = jnp.sqrt(a + EPSILON)
    behind_norm = jnp.sqrt(b + EPSILON)
    tangent_sq = jnp.maximum(
        a / (ahead_norm * ahead_norm)
        + b / (behind_norm * behind_norm)
        + 2.0 * ab / (ahead_norm * behind_norm),
        0.0,
    )
    length = jnp.sqrt(tangent_sq + EPSILON)
    unit_sq = tangent_sq / (tangent_sq + EPSILON)
    parallel = (fa / ahead_norm + fb / behind_norm) / length
    tension = spring[:, 0:1] * (ahead_norm - behind_norm)
    along = jnp.where(level > 0.5, -2.0 * parallel, tension - parallel)
    band_sq = ff + 2.0 * along * parallel + along * along * unit_sq
    inner = (row > 0) & (row < IMAGES - 1)
    force_norm = jnp.sqrt(down(jnp.where(inner, jnp.maximum(band_sq, 0.0), 0.0)) + EPSILON)
    speed_norm = jnp.sqrt(down(vv) + EPSILON)
    mine = row == image
    pick = lambda v: down(jnp.where(mine, v, 0.0))
    wide = lambda v: jnp.broadcast_to(jnp.broadcast_to(v, (1, ATOMS)), (3, ATOMS))
    energy[0] = jnp.sum(jnp.where(mine, e, 0.0))
    back = jnp.concatenate([blocks[space * BLOCK + r] for r in range(BLOCK)], axis=0)
    tangent = back[4:7] / wide(pick(ahead_norm)) + back[7:10] / wide(pick(behind_norm))
    band = back[1:4] + wide(pick(along / length)) * tangent
    speed = flat(velocity)
    mixed = wide(1.0 - mix) * speed + wide(mix * speed_norm / force_norm) * band
    kept = jnp.where(wide(reset) > 0.5, 0.0, mixed)
    movable = (image > 0) & (image < IMAGES - 1)
    speed = jnp.where(movable, kept + wide(step) * band, 0.0)
    moved = flat(pos) + wide(step) * speed
    for j in range(3):
        new_speed[j] = speed[j : j + 1]
        new_pos[j] = moved[j : j + 1]


VMEM = pl.BlockSpec(memory_space=pltpu.VMEM)
SMEM = pl.BlockSpec(memory_space=pltpu.SMEM)


def call(kernel, outs, args, scalars=(), scalar_outs=(), flops=0, limit=16 << 20):
    specs = [SMEM if i in scalars else VMEM for i in range(len(args))]
    moved = sum(a.size * a.dtype.itemsize for a in args)
    return pl.pallas_call(
        kernel,
        out_shape=[jax.ShapeDtypeStruct(s, t) for s, t in outs],
        in_specs=specs,
        out_specs=[SMEM if i in scalar_outs else VMEM for i in range(len(outs))],
        compiler_params=pltpu.CompilerParams(vmem_limit_bytes=limit),
        cost_estimate=pl.CostEstimate(flops=flops, bytes_accessed=moved, transcendentals=0),
        name=kernel.__name__,
    )(*args)


def pack_call(*args):
    return pl.pallas_call(
        pack_kernel,
        out_shape=jax.ShapeDtypeStruct((PACK_ROWS, ATOMS), BF16),
        in_specs=[pl.BlockSpec(memory_space=pltpu.HBM)] * len(args),
        out_specs=VMEM,
        scratch_shapes=[pltpu.VMEM(a.shape, a.dtype) for a in args]
        + [pltpu.SemaphoreType.DMA((len(args),))],
        compiler_params=pltpu.CompilerParams(vmem_limit_bytes=60 << 20),
        name="pack_kernel",
    )(*args)


def per_device(
    positions, velocity, embed, neighbours, send_up, send_down, climb, reset,
    filter_in, filter_out, update_weight, readout, spring, time_step, mixing,
):
    square = (ATOMS, ATOMS)
    wide = (CHANNELS, PAIRS)
    positions = positions.transpose(1, 0, 2)
    velocity = velocity.transpose(1, 0, 2)
    packed = pack_call(
        positions, embed, neighbours.T, send_up.reshape(1, ATOMS), send_down.reshape(1, ATOMS)
    )
    pack = move(packed, TO_WORKER)
    in_t, out_t, update_t, read, settings = call(
        weights_kernel,
        [((256, 128), BF16), ((256, 128), BF16), ((256, 128), BF16), (square, F32), ((8, ATOMS), F32)],
        (
            packed, filter_in, filter_out, update_weight, readout.reshape(1, CHANNELS),
            reset, spring.reshape(1), time_step.reshape(1), mixing.reshape(1),
        ),
        scalars=(5, 6, 7, 8),
        flops=10**8,
        limit=60 << 20,
    )
    list_a, list_b, send_a, send_b = call(
        lists_kernel,
        [(square, BF16), (square, BF16), ((HALO_ROWS, ATOMS), BF16), ((HALO_ROWS, ATOMS), BF16)],
        (pack,),
    )
    from_a, from_b = move(send_a, SWAP_A), move(send_b, SWAP_B)
    hot, own = call(slots_kernel, [((EXT, PAIRS), BF16), ((8, ATOMS), F32)], (pack,), flops=10**9)
    hidden, send_a, send_b, update_one, pairs, rows_one = call(
        first_kernel,
        [(square, BF16), (square, BF16), (square, BF16), (square, F32), ((8, PAIRS), F32), (wide, BF16)],
        (pack, from_a, from_b, hot, list_a, list_b, in_t, out_t, update_t),
        flops=10**9,
    )
    from_a, from_b = move(send_a, SWAP_A), move(send_b, SWAP_B)
    slope_one, slope_two, filter_two = call(
        filters_kernel,
        [(wide, BF16), (wide, BF16), (wide, F32)],
        (pairs, in_t, out_t),
        flops=10**9,
    )
    energy, grad_two, rows_two, grad_own, send_a, send_b = call(
        second_kernel,
        [((8, ATOMS), F32), (square, F32), (wide, BF16), (square, F32), (square, BF16), (square, BF16)],
        (hidden, from_a, from_b, hot, filter_two, update_t, update_weight, read),
        flops=10**9,
    )
    from_a, from_b = move(send_a, SWAP_A), move(send_b, SWAP_B)
    (dsq_two,) = call(
        slope_kernel,
        [((8, PAIRS), F32)],
        (grad_two, rows_two, slope_two, filter_out),
        flops=10**9,
    )
    force, send_a, send_b = call(
        third_kernel,
        [((8, ATOMS), F32)] * 3,
        (
            grad_own, from_a, from_b, list_a, list_b, update_one, update_weight, rows_one,
            slope_one, filter_out, dsq_two, pairs, hot,
        ),
        flops=10**9,
    )
    from_a, from_b = move(send_a, SWAP_A), move(send_b, SWAP_B)
    (blocks,) = call(
        sums_kernel,
        [((IMAGES * 8, ATOMS), F32)],
        (force, from_a, from_b, list_a, list_b, own, energy, velocity, climb),
        scalars=(8,),
    )
    column = lax.all_to_all(blocks, AXES, 0, 0, tiled=True, axis_index_groups=COLUMNS)
    (blocks,) = call(column_kernel, [((DOMAINS * BLOCK, 2, ATOMS), F32)], (column,))
    table = lax.all_to_all(blocks, AXES, 0, 0, tiled=True, axis_index_groups=LAYERS)
    new_pos, new_speed, energies = call(
        final_kernel,
        [((3, 1, ATOMS), F32), ((3, 1, ATOMS), F32), ((1,), F32)],
        (table, positions, velocity, settings),
        scalar_outs=(2,),
    )
    return new_pos.transpose(1, 0, 2), new_speed.transpose(1, 0, 2), energies


def solution(mesh):
    placed = (
        P("image", None, "space"),
        P("image", None, "space"),
        P("space", None),
        P("space", None),
        P("space"),
        P("space"),
        P("image"),
        P("image"),
    ) + (P(),) * 7
    return jax.shard_map(
        per_device,
        mesh=mesh,
        in_specs=placed,
        out_specs=(P("image", None, "space"), P("image", None, "space"), P("image")),
        check_vma=False,
    )
```

```python
import jax
import jax.numpy as jnp
from jax import lax
from jax.experimental import pallas as pl
from jax.experimental.pallas import tpu as pltpu
from jax.sharding import PartitionSpec as P

EPSILON = 1e-06
BASIS_WIDTH = 0.6
BASIS_REACH = 6.0
BASIS = 16
IMAGES = 16
DOMAINS = 32
ATOMS = 128
CHANNELS = 128
SLOTS = 32
PAIRS = ATOMS * SLOTS
CHUNK = 2048
PER_CHUNK = CHUNK // ATOMS
CHUNKS = PAIRS // CHUNK
EXT = 3 * ATOMS
AXES = ("image", "space")
F32 = jnp.float32
BF16 = jnp.bfloat16

ROW_POS = 128
ROW_AUX = 152
ROW_NEAR = 160
PACK_ROWS = 192
HALO_ROWS = 160
EXTRA = 16
BLOCK = 5


def device_at(x, y, z, core):
    return ((y * 2 + z // 8) * 2 + core) * DOMAINS + x * 8 + z % 8


def home(image, domain):
    return image * DOMAINS + domain


RING = [
    (1, 2), (1, 3), (0, 3), (0, 2), (0, 1), (0, 0), (1, 0), (1, 1),
    (2, 1), (2, 0), (3, 0), (3, 1), (3, 2), (3, 3), (2, 3), (2, 2),
]
LAYER_PAIR = (1, 0, 3, 2)


def worker(image, domain):
    x, y = RING[domain // 2]
    home_y, half, side = image // 4, image // 2 % 2, image % 2
    return device_at(x, y, half * 8 + LAYER_PAIR[home_y] * 2 + side, domain % 2)


CELLS = [(i, d) for i in range(IMAGES) for d in range(DOMAINS)]
TO_WORKER = [(home(i, d), worker(i, d)) for i, d in CELLS]
SWAP_A = [(worker(i, d), worker(i, d ^ 1)) for i, d in CELLS]
SWAP_B = [(worker(i, d), worker(i, (d + 1) % DOMAINS if d % 2 else (d - 1) % DOMAINS)) for i, d in CELLS]
LAYERS = [[worker(i, d) for d in range(DOMAINS)] for i in range(IMAGES)]
COLUMNS = [[worker(i, d) for i in range(IMAGES)] for d in range(DOMAINS)]


def move(values, pairs):
    return lax.ppermute(values, AXES, pairs)


def place():
    image, space = lax.axis_index("image"), lax.axis_index("space")
    cell = (lax.shift_right_logical(space, 3) << 2) + lax.shift_right_logical(image, 2)
    pair = jnp.int32(0)
    for step, (x, y) in enumerate(RING):
        pair = jnp.where(cell == x * 4 + y, step, pair)
    return image, lax.shift_right_logical(image, 1) & 1, pair * 2 + (image & 1)


def dot(a, b):
    return jnp.dot(a, b, preferred_element_type=F32)


def dot_nt(a, b):
    return lax.dot_general(a, b, (((1,), (1,)), ((), ())), preferred_element_type=F32)


def gate(v):
    return 0.5 * jnp.tanh(0.5 * v) + 0.5


def halves(v):
    high = v.astype(BF16)
    return high, (v - high.astype(F32)).astype(BF16)


def thirds(v):
    high = v.astype(BF16)
    rest = v - high.astype(F32)
    middle = rest.astype(BF16)
    return high, middle, (rest - middle.astype(F32)).astype(BF16)


def centres():
    step = BASIS_REACH / (BASIS - 1)
    return lax.broadcasted_iota(jnp.int32, (BASIS, CHUNK), 0).astype(F32) * step


def stacked(v):
    high, low = halves(v)
    return jnp.concatenate([high, low, high], axis=0)


def chunk(c):
    return pl.ds(c * CHUNK, CHUNK)


def fold(v):
    total = v[:, :ATOMS]
    for k in range(1, PER_CHUNK):
        total = total + v[:, k * ATOMS : (k + 1) * ATOMS]
    return total


def spread(v):
    return jnp.concatenate([v] * PER_CHUNK, axis=1)


def flat(ref):
    return jnp.concatenate([ref[0], ref[1], ref[2]], axis=0)


def spare(ref):
    rows = ref.shape[0]
    ref[rows - EXTRA : rows, :] = jnp.zeros((EXTRA, ATOMS), ref.dtype)


def coords_of(block):
    b = block[ROW_POS : ROW_POS + 24].astype(F32)
    return b[0:8] + b[8:16] + b[16:24]


def pack_kernel(
    pos_in, embed_in, near_in, up_in, down_in, out,
    pos, embed, near, up, down, sems,
):
    pairs = ((embed_in, embed), (near_in, near), (pos_in, pos), (up_in, up), (down_in, down))
    copies = [pltpu.make_async_copy(a, b, sems.at[i]) for i, (a, b) in enumerate(pairs)]
    for copy in copies:
        copy.start()
    copies[0].wait()
    out[0:CHANNELS, :] = embed[...].astype(F32).T.astype(BF16)
    copies[1].wait()
    out[ROW_NEAR:PACK_ROWS, :] = (near[...].astype(F32) - float(ATOMS)).astype(BF16)
    for copy in copies[2:]:
        copy.wait()
    zeros = jnp.zeros((5, ATOMS), F32)
    parts = [jnp.concatenate([p.astype(F32), zeros], axis=0) for p in thirds(flat(pos))]
    aux = jnp.concatenate([up[...].astype(F32), down[...].astype(F32), zeros, zeros[:1]], axis=0)
    out[ROW_POS:ROW_NEAR, :] = jnp.concatenate(parts + [aux], axis=0).astype(BF16)


def weights_kernel(
    after, filter_in, filter_out, update, readout, reset, spring, time_step, mixing,
    in_t, out_t, update_t, read, settings,
):
    for j, value in enumerate((reset[0].astype(F32), spring[0], time_step[0], mixing[0])):
        settings[j : j + 1, :] = jnp.full((1, ATOMS), value, F32)
    settings[4:8, :] = jnp.zeros((4, ATOMS), F32)
    for l in range(2):
        rows = pl.ds(l * 128, 128)
        high, low = halves(0.5 * filter_in[l])
        filler = jnp.zeros((128 - 3 * BASIS, CHANNELS), F32)
        tall = jnp.concatenate(
            [high.astype(F32), high.astype(F32), low.astype(F32), filler], axis=0
        )
        in_t[rows, :] = tall.T.astype(BF16)
        out_t[rows, :] = filter_out[l].astype(F32).T.astype(BF16)
        update_t[rows, :] = update[l].astype(F32).T.astype(BF16)
    read[...] = jnp.broadcast_to(readout[...], (CHANNELS, ATOMS)).T


def lists_kernel(pack, list_a, list_b, send_a, send_b):
    _, _, domain = place()
    even = (domain & 1) == 0
    aux = pack[ROW_AUX : ROW_AUX + 8, :].astype(F32)
    up, down = aux[0:1], aux[1:2]
    rows = lax.broadcasted_iota(jnp.int32, (ATOMS, ATOMS), 0).astype(F32)
    block = pack[0:HALO_ROWS, :]
    for ids, chosen, send in (
        (jnp.where(even, up, down), list_a, send_a),
        (jnp.where(even, down, up), list_b, send_b),
    ):
        hot = jnp.where(rows == ids, 1.0, 0.0).astype(BF16)
        chosen[...] = hot
        send[0:HALO_ROWS, :] = dot(block, hot).astype(BF16)


    spare(send_b)


def slots_kernel(pack, hot, own):
    own[...] = coords_of(pack[0:HALO_ROWS, :])
    _, _, domain = place()
    even = (domain & 1) == 0
    slots = pack[ROW_NEAR:PACK_ROWS, :].astype(F32)
    swapped = jnp.where(slots < 0.0, slots, jnp.where(slots < 128.0, slots + 128.0, slots - 128.0))
    slots = jnp.where(even, swapped, slots)
    rows = lax.broadcasted_iota(jnp.int32, (EXT, ATOMS), 0).astype(F32) - float(ATOMS)
    for k in range(SLOTS):
        hot[:, k * ATOMS : (k + 1) * ATOMS] = jnp.where(rows == slots[k : k + 1], 1.0, 0.0).astype(BF16)


def first_kernel(
    pack, from_a, from_b, hot, list_a, list_b, in_t, out_t, update_t,
    hidden, send_a, send_b, update_one, pairs, rows_one,
):
    _, _, domain = place()
    shift = jnp.where(domain == 0, -DOMAINS, jnp.where(domain == DOMAINS - 1, DOMAINS, 0)).astype(F32)
    own = coords_of(pack[0:HALO_ROWS, :])
    first = lax.broadcasted_iota(jnp.int32, (8, ATOMS), 0) == 0
    far = coords_of(from_b[0:HALO_ROWS, :]) + jnp.where(first, shift, 0.0)
    far_rows = jnp.concatenate([p.astype(F32) for p in thirds(far)], axis=0).astype(BF16)
    ext_embed = jnp.concatenate([pack[0:CHANNELS, :], from_a[0:CHANNELS, :], from_b[0:CHANNELS, :]], axis=1)
    f32_rows = lambda ref: ref[ROW_POS:HALO_ROWS, :].astype(F32)
    far_full = jnp.concatenate([far_rows.astype(F32), jnp.zeros((8, ATOMS), F32)], axis=0)
    ext_pos = jnp.concatenate([f32_rows(pack), f32_rows(from_a), far_full], axis=1).astype(BF16)
    ext = jnp.concatenate([ext_embed, ext_pos], axis=0)
    own_wide = spread(own)
    centre = centres()
    message = jnp.zeros((CHANNELS, ATOMS), F32)
    for c in range(CHUNKS):
        got = dot(ext, hot[:, chunk(c)])
        vec = got[128:136] + got[136:144] + got[144:152] - own_wide
        pairs[:, chunk(c)] = vec
        sq = jnp.sum(vec * vec, axis=0, keepdims=True)
        scaled = (sq - centre) * (1.0 / BASIS_WIDTH)
        radial = jnp.exp(-scaled * scaled)
        half = dot(in_t[0:128, 0 : 3 * BASIS], stacked(radial))
        act = (half + half * jnp.tanh(half)).astype(BF16)
        filt = dot(out_t[0:128, :], act)
        rows = got[0:CHANNELS]
        rows_one[:, chunk(c)] = rows.astype(BF16)
        message = message + fold(filt * rows)
    upd = dot(update_t[0:128, :], message.astype(BF16))
    update_one[...] = upd
    hid = (pack[0:CHANNELS, :].astype(F32) + upd * gate(upd)).astype(BF16)
    hidden[...] = hid
    send_a[...] = dot(hid, list_a[...]).astype(BF16)
    send_b[0:CHANNELS, :] = dot(hid, list_b[...]).astype(BF16)
    spare(send_b)


def bend(pairs, in_t, layer, c, centre):
    vec = pairs[:, chunk(c)]
    sq = jnp.sum(vec * vec, axis=0, keepdims=True)
    scaled = (sq - centre) * (1.0 / BASIS_WIDTH)
    radial = jnp.exp(-scaled * scaled)
    weight = in_t[layer * 128 : (layer + 1) * 128, 0 : 3 * BASIS]
    half = dot(weight, stacked(radial))
    change = dot(weight, stacked(radial * scaled * (-2.0 / BASIS_WIDTH)))
    t = jnp.tanh(half)
    bent = half * t
    return half + bent, (1.0 + t) * (1.0 + half - bent) * change


def filters_kernel(pairs, in_t, out_t, slope_two, filter_two):
    centre = centres()
    for c in range(CHUNKS):
        act, slope = bend(pairs, in_t, 1, c, centre)
        slope_two[:, chunk(c)] = slope.astype(BF16)
        filter_two[:, chunk(c)] = dot(out_t[128:256, :], act.astype(BF16))


def second_kernel(
    hidden, from_a, from_b, hot, filter_two, update_t, update, read,
    energy, grad_two, rows_two, grad_own, grad_a, grad_b,
):
    ext = jnp.concatenate([hidden[...], from_a[...], from_b[0:CHANNELS, :]], axis=1)
    message = jnp.zeros((CHANNELS, ATOMS), F32)
    for c in range(CHUNKS):
        rows = dot(ext, hot[:, chunk(c)])
        rows_two[:, chunk(c)] = rows.astype(BF16)
        message = message + fold(filter_two[:, chunk(c)] * rows)
    upd = dot(update_t[128:256, :], message.astype(BF16))
    g = gate(upd)
    act = upd * g
    weight = read[...]
    energy[...] = jnp.broadcast_to(jnp.sum(act * weight, axis=0, keepdims=True), (8, ATOMS))
    dupd = ((g + act * (1.0 - g)) * weight).astype(BF16)
    grad = dot(update[1], dupd)
    grad_two[...] = grad
    wide = spread(grad)
    total = jnp.zeros((CHANNELS, EXT), F32)
    for c in range(CHUNKS):
        part = (filter_two[:, chunk(c)] * wide).astype(BF16)
        total = total + dot_nt(part, hot[:, chunk(c)])
    grad_own[...] = total[:, 0:ATOMS]
    grad_a[...] = total[:, ATOMS : 2 * ATOMS].astype(BF16)
    grad_b[0:CHANNELS, :] = total[:, 2 * ATOMS :].astype(BF16)
    spare(grad_b)


def slope_kernel(grad_two, rows_two, slope_two, filter_out, pairs, in_t, out, slope_one):
    centre = centres()
    wide = spread(grad_two[...])
    for c in range(CHUNKS):
        dfilt = (wide * rows_two[:, chunk(c)].astype(F32)).astype(BF16)
        dact = dot(filter_out[1], dfilt)
        part = jnp.sum(dact * slope_two[:, chunk(c)].astype(F32), axis=0, keepdims=True)
        out[:, chunk(c)] = jnp.broadcast_to(part, (8, CHUNK))
        slope_one[:, chunk(c)] = bend(pairs, in_t, 0, c, centre)[1].astype(BF16)


def third_kernel(
    grad_own, from_a, from_b, list_a, list_b, update_one, update, rows_one, slope_one,
    filter_out, dsq_two, pairs, hot,
    force, send_a, send_b,
):
    dhidden = grad_own[...] + dot_nt(from_a[...], list_a[...]) + dot_nt(from_b[0:CHANNELS, :], list_b[...])
    upd = update_one[...]
    g = gate(upd)
    dupd = (dhidden * (g + upd * g * (1.0 - g))).astype(BF16)
    wide = spread(dot(update[0], dupd))
    own = jnp.zeros((8, ATOMS), F32)
    total = jnp.zeros((16, EXT), F32)
    for c in range(CHUNKS):
        dfilt = (wide * rows_one[:, chunk(c)].astype(F32)).astype(BF16)
        dact = dot(filter_out[0], dfilt)
        part = jnp.sum(dact * slope_one[:, chunk(c)].astype(F32), axis=0, keepdims=True)
        pull = 2.0 * (part + dsq_two[:, chunk(c)]) * pairs[:, chunk(c)]
        own = own + fold(pull)
        high, low = halves(pull)
        both = jnp.concatenate([high.astype(F32), low.astype(F32)], axis=0).astype(BF16)
        total = total + dot_nt(both, hot[:, chunk(c)])
    ext = total[0:8] + total[8:16]
    force[...] = own - ext[:, 0:ATOMS]
    send_a[...] = -ext[:, ATOMS : 2 * ATOMS]
    send_b[0:8, :] = -ext[:, 2 * ATOMS :]
    spare(send_b)


def sums_kernel(force, from_a, from_b, list_a, list_b, own, energy, velocity, climb, out):
    image, _, _ = place()

    def returned(block, chosen):
        both = jnp.concatenate([p.astype(F32) for p in halves(block)], axis=0).astype(BF16)
        got = dot_nt(both, chosen)
        return got[0:8] + got[8:16]

    f = force[...] + returned(from_a[...], list_a[...]) + returned(from_b[0:8, :], list_b[...])
    speed = flat(velocity)
    movable = (image > 0) & (image < IMAGES - 1)
    speed_sq = jnp.where(movable, jnp.sum(speed * speed), 0.0)
    lane = lax.broadcasted_iota(jnp.int32, (1, ATOMS), 1)
    last = jnp.where(lane == 6 * IMAGES, speed_sq, 0.0)
    last = jnp.where(lane == 7 * IMAGES + image, climb[0].astype(F32), last)
    block = jnp.concatenate([f[0:3], own[0:3, :], energy[0:1, :], last], axis=0)
    for j in range(IMAGES):
        out[j * 8 : (j + 1) * 8, :] = block


def column_kernel(blocks, out):
    _, half, _ = place()
    part = lambda r: blocks[pl.ds(r, IMAGES, stride=8), :]
    force = [part(r) for r in range(3)]
    coords = [part(r + 3) for r in range(3)]
    ahead = [jnp.concatenate([p[1:], p[-1:]], axis=0) - p for p in coords]
    behind = [p - jnp.concatenate([p[:1], p[:-1]], axis=0) for p in coords]
    inner = lambda u, v: u[0] * v[0] + u[1] * v[1] + u[2] * v[2]
    rows = [
        part(6),
        inner(ahead, ahead),
        inner(ahead, behind),
        inner(force, ahead),
        inner(force, behind),
        inner(force, force),
        jnp.zeros((2 * IMAGES, ATOMS), F32),
    ]
    square = jnp.concatenate(rows, axis=0)
    table = jnp.sum(square.T, axis=0, keepdims=True) + jnp.sum(part(7), axis=0, keepdims=True)
    parts = force + ahead + behind
    for y in range(4):
        for core in range(2):
            low = y * 4 + core
            pick = lambda v: jnp.where(half == 0, v[low : low + 1], v[low + 2 : low + 3])
            lines = [table] + [pick(v) for v in parts]
            pairs = [jnp.concatenate(lines[2 * r : 2 * r + 2], axis=0) for r in range(BLOCK)]
            for x in range(4):
                target = RING.index((x, y)) * 2 + core
                for r in range(BLOCK):
                    out[target * BLOCK + r] = pairs[r]


def final_kernel(blocks, pos, velocity, settings, new_pos, new_speed, energy):
    image, _, _ = place()
    space = lax.axis_index("space")
    reset, spring, step, mix = (settings[j : j + 1, :] for j in range(4))
    total = blocks[0]
    for j in range(1, DOMAINS):
        total = total + blocks[j * BLOCK]
    row = lax.broadcasted_iota(jnp.int32, (IMAGES, 1), 0)
    lane = lax.broadcasted_iota(jnp.int32, (IMAGES, ATOMS), 1)
    table = jnp.broadcast_to(total[0:1], (IMAGES, ATOMS))
    column = lambda j: jnp.sum(jnp.where(lane == row + j * IMAGES, table, 0.0), axis=1, keepdims=True)
    e, a, ab, fa, fb, ff, vv, level = (column(j) for j in range(8))
    b = jnp.concatenate([a[:1], a[:-1]], axis=0)
    down = lambda v: jnp.sum(v, axis=0, keepdims=True)
    ahead_norm = jnp.sqrt(a + EPSILON)
    behind_norm = jnp.sqrt(b + EPSILON)
    tangent_sq = jnp.maximum(
        a / (ahead_norm * ahead_norm)
        + b / (behind_norm * behind_norm)
        + 2.0 * ab / (ahead_norm * behind_norm),
        0.0,
    )
    length = jnp.sqrt(tangent_sq + EPSILON)
    unit_sq = tangent_sq / (tangent_sq + EPSILON)
    parallel = (fa / ahead_norm + fb / behind_norm) / length
    tension = spring[:, 0:1] * (ahead_norm - behind_norm)
    along = jnp.where(level > 0.5, -2.0 * parallel, tension - parallel)
    band_sq = ff + 2.0 * along * parallel + along * along * unit_sq
    inner = (row > 0) & (row < IMAGES - 1)
    force_norm = jnp.sqrt(down(jnp.where(inner, jnp.maximum(band_sq, 0.0), 0.0)) + EPSILON)
    speed_norm = jnp.sqrt(down(vv) + EPSILON)
    mine = row == image
    pick = lambda v: down(jnp.where(mine, v, 0.0))
    wide = lambda v: jnp.broadcast_to(jnp.broadcast_to(v, (1, ATOMS)), (3, ATOMS))
    energy[0] = jnp.sum(jnp.where(mine, e, 0.0))
    back = jnp.concatenate([blocks[space * BLOCK + r] for r in range(BLOCK)], axis=0)
    tangent = back[4:7] / wide(pick(ahead_norm)) + back[7:10] / wide(pick(behind_norm))
    band = back[1:4] + wide(pick(along / length)) * tangent
    speed = flat(velocity)
    mixed = wide(1.0 - mix) * speed + wide(mix * speed_norm / force_norm) * band
    kept = jnp.where(wide(reset) > 0.5, 0.0, mixed)
    movable = (image > 0) & (image < IMAGES - 1)
    speed = jnp.where(movable, kept + wide(step) * band, 0.0)
    moved = flat(pos) + wide(step) * speed
    for j in range(3):
        new_speed[j] = speed[j : j + 1]
        new_pos[j] = moved[j : j + 1]


VMEM = pl.BlockSpec(memory_space=pltpu.VMEM)
SMEM = pl.BlockSpec(memory_space=pltpu.SMEM)


def call(kernel, outs, args, scalars=(), scalar_outs=(), flops=0, limit=16 << 20):
    specs = [SMEM if i in scalars else VMEM for i in range(len(args))]
    moved = sum(a.size * a.dtype.itemsize for a in args)
    return pl.pallas_call(
        kernel,
        out_shape=[jax.ShapeDtypeStruct(s, t) for s, t in outs],
        in_specs=specs,
        out_specs=[SMEM if i in scalar_outs else VMEM for i in range(len(outs))],
        compiler_params=pltpu.CompilerParams(vmem_limit_bytes=limit),
        cost_estimate=pl.CostEstimate(flops=flops, bytes_accessed=moved, transcendentals=0),
        name=kernel.__name__,
    )(*args)


def pack_call(*args):
    return pl.pallas_call(
        pack_kernel,
        out_shape=jax.ShapeDtypeStruct((PACK_ROWS, ATOMS), BF16),
        in_specs=[pl.BlockSpec(memory_space=pltpu.HBM)] * len(args),
        out_specs=VMEM,
        scratch_shapes=[pltpu.VMEM(a.shape, a.dtype) for a in args]
        + [pltpu.SemaphoreType.DMA((len(args),))],
        compiler_params=pltpu.CompilerParams(vmem_limit_bytes=60 << 20),
        name="pack_kernel",
    )(*args)


def per_device(
    positions, velocity, embed, neighbours, send_up, send_down, climb, reset,
    filter_in, filter_out, update_weight, readout, spring, time_step, mixing,
):
    square = (ATOMS, ATOMS)
    wide = (CHANNELS, PAIRS)
    longer = (CHANNELS + EXTRA, ATOMS)
    positions = positions.transpose(1, 0, 2)
    velocity = velocity.transpose(1, 0, 2)
    packed = pack_call(
        positions, embed, neighbours.T, send_up.reshape(1, ATOMS), send_down.reshape(1, ATOMS)
    )
    pack = move(packed, TO_WORKER)
    in_t, out_t, update_t, read, settings = call(
        weights_kernel,
        [((256, 128), BF16), ((256, 128), BF16), ((256, 128), BF16), (square, F32), ((8, ATOMS), F32)],
        (
            packed, filter_in, filter_out, update_weight, readout.reshape(1, CHANNELS),
            reset, spring.reshape(1), time_step.reshape(1), mixing.reshape(1),
        ),
        scalars=(5, 6, 7, 8),
        flops=10**8,
        limit=60 << 20,
    )
    list_a, list_b, send_a, send_b = call(
        lists_kernel,
        [(square, BF16), (square, BF16), ((HALO_ROWS, ATOMS), BF16), ((HALO_ROWS + EXTRA, ATOMS), BF16)],
        (pack,),
    )
    from_b, from_a = move(send_b, SWAP_B), move(send_a, SWAP_A)
    hot, own = call(slots_kernel, [((EXT, PAIRS), BF16), ((8, ATOMS), F32)], (pack,), flops=10**9)
    hidden, send_a, send_b, update_one, pairs, rows_one = call(
        first_kernel,
        [(square, BF16), (square, BF16), (longer, BF16), (square, F32), ((8, PAIRS), F32), (wide, BF16)],
        (pack, from_a, from_b, hot, list_a, list_b, in_t, out_t, update_t),
        flops=10**9,
    )
    from_b, from_a = move(send_b, SWAP_B), move(send_a, SWAP_A)
    slope_two, filter_two = call(
        filters_kernel,
        [(wide, BF16), (wide, F32)],
        (pairs, in_t, out_t),
        flops=10**9,
    )
    energy, grad_two, rows_two, grad_own, send_a, send_b = call(
        second_kernel,
        [((8, ATOMS), F32), (square, F32), (wide, BF16), (square, F32), (square, BF16), (longer, BF16)],
        (hidden, from_a, from_b, hot, filter_two, update_t, update_weight, read),
        flops=10**9,
    )
    from_b, from_a = move(send_b, SWAP_B), move(send_a, SWAP_A)
    dsq_two, slope_one = call(
        slope_kernel,
        [((8, PAIRS), F32), (wide, BF16)],
        (grad_two, rows_two, slope_two, filter_out, pairs, in_t),
        flops=10**9,
    )
    force, send_a, send_b = call(
        third_kernel,
        [((8, ATOMS), F32), ((8, ATOMS), F32), ((8 + EXTRA, ATOMS), F32)],
        (
            grad_own, from_a, from_b, list_a, list_b, update_one, update_weight, rows_one,
            slope_one, filter_out, dsq_two, pairs, hot,
        ),
        flops=10**9,
    )
    from_b, from_a = move(send_b, SWAP_B), move(send_a, SWAP_A)
    (blocks,) = call(
        sums_kernel,
        [((IMAGES * 8, ATOMS), F32)],
        (force, from_a, from_b, list_a, list_b, own, energy, velocity, climb),
        scalars=(8,),
    )
    column = lax.all_to_all(blocks, AXES, 0, 0, tiled=True, axis_index_groups=COLUMNS)
    (blocks,) = call(column_kernel, [((DOMAINS * BLOCK, 2, ATOMS), F32)], (column,))
    table = lax.all_to_all(blocks, AXES, 0, 0, tiled=True, axis_index_groups=LAYERS)
    new_pos, new_speed, energies = call(
        final_kernel,
        [((3, 1, ATOMS), F32), ((3, 1, ATOMS), F32), ((1,), F32)],
        (table, positions, velocity, settings),
        scalar_outs=(2,),
    )
    return new_pos.transpose(1, 0, 2), new_speed.transpose(1, 0, 2), energies


def solution(mesh):
    placed = (
        P("image", None, "space"),
        P("image", None, "space"),
        P("space", None),
        P("space", None),
        P("space"),
        P("space"),
        P("image"),
        P("image"),
    ) + (P(),) * 7
    return jax.shard_map(
        per_device,
        mesh=mesh,
        in_specs=placed,
        out_specs=(P("image", None, "space"), P("image", None, "space"), P("image")),
        check_vma=False,
    )
```

```python
import jax
import jax.numpy as jnp
from jax import lax
from jax.experimental import pallas as pl
from jax.experimental.pallas import tpu as pltpu
from jax.sharding import PartitionSpec as P

EPSILON = 1e-06
BASIS_WIDTH = 0.6
BASIS_REACH = 6.0
BASIS = 16
IMAGES = 16
DOMAINS = 32
ATOMS = 128
CHANNELS = 128
SLOTS = 32
PAIRS = ATOMS * SLOTS
CHUNK = 2048
PER_CHUNK = CHUNK // ATOMS
CHUNKS = PAIRS // CHUNK
EXT = 3 * ATOMS
AXES = ("image", "space")
F32 = jnp.float32
BF16 = jnp.bfloat16

ROW_POS = 128
ROW_AUX = 152
ROW_NEAR = 160
PACK_ROWS = 192
HALO_ROWS = 160
EXTRA = 16
BLOCK = 5


def device_at(x, y, z, core):
    return ((y * 2 + z // 8) * 2 + core) * DOMAINS + x * 8 + z % 8


def home(image, domain):
    return image * DOMAINS + domain


RING = [
    (1, 2), (1, 3), (0, 3), (0, 2), (0, 1), (0, 0), (1, 0), (1, 1),
    (2, 1), (2, 0), (3, 0), (3, 1), (3, 2), (3, 3), (2, 3), (2, 2),
]
LAYER_PAIR = (1, 0, 3, 2)


def worker(image, domain):
    x, y = RING[domain // 2]
    home_y, half, side = image // 4, image // 2 % 2, image % 2
    return device_at(x, y, half * 8 + LAYER_PAIR[home_y] * 2 + side, domain % 2)


CELLS = [(i, d) for i in range(IMAGES) for d in range(DOMAINS)]
TO_WORKER = [(home(i, d), worker(i, d)) for i, d in CELLS]
SWAP_A = [(worker(i, d), worker(i, d ^ 1)) for i, d in CELLS]
SWAP_B = [(worker(i, d), worker(i, (d + 1) % DOMAINS if d % 2 else (d - 1) % DOMAINS)) for i, d in CELLS]
LAYERS = [[worker(i, d) for d in range(DOMAINS)] for i in range(IMAGES)]
COLUMNS = [[worker(i, d) for i in range(IMAGES)] for d in range(DOMAINS)]


def move(values, pairs):
    return lax.ppermute(values, AXES, pairs)


def place():
    image, space = lax.axis_index("image"), lax.axis_index("space")
    cell = (lax.shift_right_logical(space, 3) << 2) + lax.shift_right_logical(image, 2)
    pair = jnp.int32(0)
    for step, (x, y) in enumerate(RING):
        pair = jnp.where(cell == x * 4 + y, step, pair)
    return image, lax.shift_right_logical(image, 1) & 1, pair * 2 + (image & 1)


def dot(a, b):
    return jnp.dot(a, b, preferred_element_type=F32)


def dot_nt(a, b):
    return lax.dot_general(a, b, (((1,), (1,)), ((), ())), preferred_element_type=F32)


def gate(v):
    return 0.5 * jnp.tanh(0.5 * v) + 0.5


def halves(v):
    high = v.astype(BF16)
    return high, (v - high.astype(F32)).astype(BF16)


def thirds(v):
    high = v.astype(BF16)
    rest = v - high.astype(F32)
    middle = rest.astype(BF16)
    return high, middle, (rest - middle.astype(F32)).astype(BF16)


def centres():
    step = BASIS_REACH / (BASIS - 1)
    return lax.broadcasted_iota(jnp.int32, (BASIS, CHUNK), 0).astype(F32) * step


def stacked(v):
    high, low = halves(v)
    return jnp.concatenate([high, low, high], axis=0)


def chunk(c):
    return pl.ds(c * CHUNK, CHUNK)


def fold(v):
    total = v[:, :ATOMS]
    for k in range(1, PER_CHUNK):
        total = total + v[:, k * ATOMS : (k + 1) * ATOMS]
    return total


def spread(v):
    return jnp.concatenate([v] * PER_CHUNK, axis=1)


def flat(ref):
    return jnp.concatenate([ref[0], ref[1], ref[2]], axis=0)


def spare(ref):
    rows = ref.shape[0]
    ref[rows - EXTRA : rows, :] = jnp.zeros((EXTRA, ATOMS), ref.dtype)


def coords_of(block):
    b = block[ROW_POS : ROW_POS + 24].astype(F32)
    return b[0:8] + b[8:16] + b[16:24]


def pack_kernel(
    pos_in, embed_in, near_in, up_in, down_in, out,
    pos, embed, near, up, down, sems,
):
    pairs = ((embed_in, embed), (near_in, near), (pos_in, pos), (up_in, up), (down_in, down))
    copies = [pltpu.make_async_copy(a, b, sems.at[i]) for i, (a, b) in enumerate(pairs)]
    for copy in copies:
        copy.start()
    copies[0].wait()
    out[0:CHANNELS, :] = embed[...].astype(F32).T.astype(BF16)
    copies[1].wait()
    out[ROW_NEAR:PACK_ROWS, :] = (near[...].astype(F32) - float(ATOMS)).astype(BF16)
    for copy in copies[2:]:
        copy.wait()
    zeros = jnp.zeros((5, ATOMS), F32)
    parts = [jnp.concatenate([p.astype(F32), zeros], axis=0) for p in thirds(flat(pos))]
    aux = jnp.concatenate([up[...].astype(F32), down[...].astype(F32), zeros, zeros[:1]], axis=0)
    out[ROW_POS:ROW_NEAR, :] = jnp.concatenate(parts + [aux], axis=0).astype(BF16)


def weights_kernel(
    after, filter_in, filter_out, update, readout, reset, spring, time_step, mixing,
    in_t, out_t, update_t, read, settings,
):
    for j, value in enumerate((reset[0].astype(F32), spring[0], time_step[0], mixing[0])):
        settings[j : j + 1, :] = jnp.full((1, ATOMS), value, F32)
    settings[4:8, :] = jnp.zeros((4, ATOMS), F32)
    for l in range(2):
        rows = pl.ds(l * 128, 128)
        high, low = halves(0.5 * filter_in[l])
        filler = jnp.zeros((128 - 3 * BASIS, CHANNELS), F32)
        tall = jnp.concatenate(
            [high.astype(F32), high.astype(F32), low.astype(F32), filler], axis=0
        )
        in_t[rows, :] = tall.T.astype(BF16)
        out_t[rows, :] = filter_out[l].astype(F32).T.astype(BF16)
        update_t[rows, :] = update[l].astype(F32).T.astype(BF16)
    read[...] = jnp.broadcast_to(readout[...], (CHANNELS, ATOMS)).T


def lists_kernel(pack, list_a, list_b, send_a, send_b):
    _, _, domain = place()
    even = (domain & 1) == 0
    aux = pack[ROW_AUX : ROW_AUX + 8, :].astype(F32)
    up, down = aux[0:1], aux[1:2]
    rows = lax.broadcasted_iota(jnp.int32, (ATOMS, ATOMS), 0).astype(F32)
    block = pack[0:HALO_ROWS, :]
    for ids, chosen, send in (
        (jnp.where(even, up, down), list_a, send_a),
        (jnp.where(even, down, up), list_b, send_b),
    ):
        hot = jnp.where(rows == ids, 1.0, 0.0).astype(BF16)
        chosen[...] = hot
        send[0:HALO_ROWS, :] = dot(block, hot).astype(BF16)


    spare(send_b)


def slots_kernel(pack, hot, own):
    own[...] = coords_of(pack[0:HALO_ROWS, :])
    _, _, domain = place()
    even = (domain & 1) == 0
    slots = pack[ROW_NEAR:PACK_ROWS, :].astype(F32)
    swapped = jnp.where(slots < 0.0, slots, jnp.where(slots < 128.0, slots + 128.0, slots - 128.0))
    slots = jnp.where(even, swapped, slots)
    rows = lax.broadcasted_iota(jnp.int32, (EXT, ATOMS), 0).astype(F32) - float(ATOMS)
    for k in range(SLOTS):
        hot[:, k * ATOMS : (k + 1) * ATOMS] = jnp.where(rows == slots[k : k + 1], 1.0, 0.0).astype(BF16)


def first_kernel(
    pack, from_a, from_b, hot, list_a, list_b, in_t, out_t, update_t,
    hidden, send_a, send_b, update_one, pairs, rows_one,
):
    _, _, domain = place()
    shift = jnp.where(domain == 0, -DOMAINS, jnp.where(domain == DOMAINS - 1, DOMAINS, 0)).astype(F32)
    own = coords_of(pack[0:HALO_ROWS, :])
    first = lax.broadcasted_iota(jnp.int32, (8, ATOMS), 0) == 0
    far = coords_of(from_b[0:HALO_ROWS, :]) + jnp.where(first, shift, 0.0)
    far_rows = jnp.concatenate([p.astype(F32) for p in thirds(far)], axis=0).astype(BF16)
    ext_embed = jnp.concatenate([pack[0:CHANNELS, :], from_a[0:CHANNELS, :], from_b[0:CHANNELS, :]], axis=1)
    f32_rows = lambda ref: ref[ROW_POS:HALO_ROWS, :].astype(F32)
    far_full = jnp.concatenate([far_rows.astype(F32), jnp.zeros((8, ATOMS), F32)], axis=0)
    ext_pos = jnp.concatenate([f32_rows(pack), f32_rows(from_a), far_full], axis=1).astype(BF16)
    ext = jnp.concatenate([ext_embed, ext_pos], axis=0)
    own_wide = spread(own)
    centre = centres()
    message = jnp.zeros((CHANNELS, ATOMS), F32)
    for c in range(CHUNKS):
        got = dot(ext, hot[:, chunk(c)])
        vec = got[128:136] + got[136:144] + got[144:152] - own_wide
        pairs[:, chunk(c)] = vec
        sq = jnp.sum(vec * vec, axis=0, keepdims=True)
        scaled = (sq - centre) * (1.0 / BASIS_WIDTH)
        radial = jnp.exp(-scaled * scaled)
        half = dot(in_t[0:128, 0 : 3 * BASIS], stacked(radial))
        act = (half + half * jnp.tanh(half)).astype(BF16)
        filt = dot(out_t[0:128, :], act)
        rows = got[0:CHANNELS]
        rows_one[:, chunk(c)] = rows.astype(BF16)
        message = message + fold(filt * rows)
    upd = dot(update_t[0:128, :], message.astype(BF16))
    update_one[...] = upd
    hid = (pack[0:CHANNELS, :].astype(F32) + upd * gate(upd)).astype(BF16)
    hidden[...] = hid
    send_a[...] = dot(hid, list_a[...]).astype(BF16)
    send_b[0:CHANNELS, :] = dot(hid, list_b[...]).astype(BF16)
    spare(send_b)


def bend(pairs, in_t, layer, c, centre):
    vec = pairs[:, chunk(c)]
    sq = jnp.sum(vec * vec, axis=0, keepdims=True)
    scaled = (sq - centre) * (1.0 / BASIS_WIDTH)
    radial = jnp.exp(-scaled * scaled)
    weight = in_t[layer * 128 : (layer + 1) * 128, 0 : 3 * BASIS]
    half = dot(weight, stacked(radial))
    change = dot(weight, stacked(radial * scaled * (-2.0 / BASIS_WIDTH)))
    t = jnp.tanh(half)
    bent = half * t
    return half + bent, (1.0 + t) * (1.0 + half - bent) * change


def filters_kernel(pairs, in_t, out_t, slope_two, filter_two):
    centre = centres()
    for c in range(CHUNKS):
        act, slope = bend(pairs, in_t, 1, c, centre)
        slope_two[:, chunk(c)] = slope.astype(BF16)
        filter_two[:, chunk(c)] = dot(out_t[128:256, :], act.astype(BF16))


def second_kernel(
    hidden, from_a, from_b, hot, filter_two, update_t, update, read,
    energy, grad_two, rows_two, grad_own, grad_a, grad_b,
):
    ext = jnp.concatenate([hidden[...], from_a[...], from_b[0:CHANNELS, :]], axis=1)
    message = jnp.zeros((CHANNELS, ATOMS), F32)
    for c in range(CHUNKS):
        rows = dot(ext, hot[:, chunk(c)])
        rows_two[:, chunk(c)] = rows.astype(BF16)
        message = message + fold(filter_two[:, chunk(c)] * rows)
    upd = dot(update_t[128:256, :], message.astype(BF16))
    g = gate(upd)
    act = upd * g
    weight = read[...]
    energy[...] = jnp.broadcast_to(jnp.sum(act * weight, axis=0, keepdims=True), (8, ATOMS))
    dupd = ((g + act * (1.0 - g)) * weight).astype(BF16)
    grad = dot(update[1], dupd)
    grad_two[...] = grad
    wide = spread(grad)
    total = jnp.zeros((CHANNELS, EXT), F32)
    for c in range(CHUNKS):
        part = (filter_two[:, chunk(c)] * wide).astype(BF16)
        total = total + dot_nt(part, hot[:, chunk(c)])
    grad_own[...] = total[:, 0:ATOMS]
    grad_a[...] = total[:, ATOMS : 2 * ATOMS].astype(BF16)
    grad_b[0:CHANNELS, :] = total[:, 2 * ATOMS :].astype(BF16)
    spare(grad_b)


def slope_kernel(
    grad_two, rows_two, slope_two, filter_out, pairs, in_t, out_t, rows_one, out, pull_one
):
    centre = centres()
    wide = spread(grad_two[...].astype(BF16))
    for c in range(CHUNKS):
        dfilt = wide * rows_two[:, chunk(c)]
        dact = dot(filter_out[1], dfilt)
        part = jnp.sum(dact * slope_two[:, chunk(c)].astype(F32), axis=0, keepdims=True)
        out[:, chunk(c)] = jnp.broadcast_to(part, (8, CHUNK))
        turned = dot(out_t[0:128, :], bend(pairs, in_t, 0, c, centre)[1].astype(BF16))
        pull_one[:, chunk(c)] = turned * rows_one[:, chunk(c)].astype(F32)


def third_kernel(
    grad_own, from_a, from_b, list_a, list_b, update_one, update, pull_one, dsq_two, pairs, hot,
    force, send_a, send_b,
):
    dhidden = grad_own[...] + dot_nt(from_a[...], list_a[...]) + dot_nt(from_b[0:CHANNELS, :], list_b[...])
    upd = update_one[...]
    g = gate(upd)
    dupd = (dhidden * (g + upd * g * (1.0 - g))).astype(BF16)
    wide = spread(dot(update[0], dupd))
    own = jnp.zeros((8, ATOMS), F32)
    total = jnp.zeros((16, EXT), F32)
    for c in range(CHUNKS):
        part = jnp.sum(wide * pull_one[:, chunk(c)], axis=0, keepdims=True)
        pull = 2.0 * (part + dsq_two[:, chunk(c)]) * pairs[:, chunk(c)]
        own = own + fold(pull)
        high, low = halves(pull)
        both = jnp.concatenate([high.astype(F32), low.astype(F32)], axis=0).astype(BF16)
        total = total + dot_nt(both, hot[:, chunk(c)])
    ext = total[0:8] + total[8:16]
    force[...] = own - ext[:, 0:ATOMS]
    send_a[...] = -ext[:, ATOMS : 2 * ATOMS]
    send_b[0:8, :] = -ext[:, 2 * ATOMS :]
    spare(send_b)


def sums_kernel(force, from_a, from_b, list_a, list_b, own, energy, velocity, climb, out):
    image, _, _ = place()

    def returned(block, chosen):
        both = jnp.concatenate([p.astype(F32) for p in halves(block)], axis=0).astype(BF16)
        got = dot_nt(both, chosen)
        return got[0:8] + got[8:16]

    f = force[...] + returned(from_a[...], list_a[...]) + returned(from_b[0:8, :], list_b[...])
    speed = flat(velocity)
    movable = (image > 0) & (image < IMAGES - 1)
    speed_sq = jnp.where(movable, jnp.sum(speed * speed), 0.0)
    lane = lax.broadcasted_iota(jnp.int32, (1, ATOMS), 1)
    last = jnp.where(lane == 6 * IMAGES, speed_sq, 0.0)
    last = jnp.where(lane == 7 * IMAGES + image, climb[0].astype(F32), last)
    block = jnp.concatenate([f[0:3], own[0:3, :], energy[0:1, :], last], axis=0)
    for j in range(IMAGES):
        out[j * 8 : (j + 1) * 8, :] = block


def column_kernel(blocks, out):
    _, half, _ = place()
    part = lambda r: blocks[pl.ds(r, IMAGES, stride=8), :]
    force = [part(r) for r in range(3)]
    coords = [part(r + 3) for r in range(3)]
    ahead = [jnp.concatenate([p[1:], p[-1:]], axis=0) - p for p in coords]
    behind = [p - jnp.concatenate([p[:1], p[:-1]], axis=0) for p in coords]
    inner = lambda u, v: u[0] * v[0] + u[1] * v[1] + u[2] * v[2]
    rows = [
        part(6),
        inner(ahead, ahead),
        inner(ahead, behind),
        inner(force, ahead),
        inner(force, behind),
        inner(force, force),
        jnp.zeros((2 * IMAGES, ATOMS), F32),
    ]
    square = jnp.concatenate(rows, axis=0)
    table = jnp.sum(square.T, axis=0, keepdims=True) + jnp.sum(part(7), axis=0, keepdims=True)
    parts = force + ahead + behind
    for y in range(4):
        for core in range(2):
            low = y * 4 + core
            pick = lambda v: jnp.where(half == 0, v[low : low + 1], v[low + 2 : low + 3])
            lines = [table] + [pick(v) for v in parts]
            pairs = [jnp.concatenate(lines[2 * r : 2 * r + 2], axis=0) for r in range(BLOCK)]
            for x in range(4):
                target = RING.index((x, y)) * 2 + core
                for r in range(BLOCK):
                    out[target * BLOCK + r] = pairs[r]


def final_kernel(blocks, pos, velocity, settings, new_pos, new_speed, energy):
    image, _, _ = place()
    space = lax.axis_index("space")
    reset, spring, step, mix = (settings[j : j + 1, :] for j in range(4))
    total = blocks[0]
    for j in range(1, DOMAINS):
        total = total + blocks[j * BLOCK]
    row = lax.broadcasted_iota(jnp.int32, (IMAGES, 1), 0)
    lane = lax.broadcasted_iota(jnp.int32, (IMAGES, ATOMS), 1)
    table = jnp.broadcast_to(total[0:1], (IMAGES, ATOMS))
    column = lambda j: jnp.sum(jnp.where(lane == row + j * IMAGES, table, 0.0), axis=1, keepdims=True)
    e, a, ab, fa, fb, ff, vv, level = (column(j) for j in range(8))
    b = jnp.concatenate([a[:1], a[:-1]], axis=0)
    down = lambda v: jnp.sum(v, axis=0, keepdims=True)
    ahead_norm = jnp.sqrt(a + EPSILON)
    behind_norm = jnp.sqrt(b + EPSILON)
    tangent_sq = jnp.maximum(
        a / (ahead_norm * ahead_norm)
        + b / (behind_norm * behind_norm)
        + 2.0 * ab / (ahead_norm * behind_norm),
        0.0,
    )
    length = jnp.sqrt(tangent_sq + EPSILON)
    unit_sq = tangent_sq / (tangent_sq + EPSILON)
    parallel = (fa / ahead_norm + fb / behind_norm) / length
    tension = spring[:, 0:1] * (ahead_norm - behind_norm)
    along = jnp.where(level > 0.5, -2.0 * parallel, tension - parallel)
    band_sq = ff + 2.0 * along * parallel + along * along * unit_sq
    inner = (row > 0) & (row < IMAGES - 1)
    force_norm = jnp.sqrt(down(jnp.where(inner, jnp.maximum(band_sq, 0.0), 0.0)) + EPSILON)
    speed_norm = jnp.sqrt(down(vv) + EPSILON)
    mine = row == image
    pick = lambda v: down(jnp.where(mine, v, 0.0))
    wide = lambda v: jnp.broadcast_to(jnp.broadcast_to(v, (1, ATOMS)), (3, ATOMS))
    energy[0] = jnp.sum(jnp.where(mine, e, 0.0))
    back = jnp.concatenate([blocks[space * BLOCK + r] for r in range(BLOCK)], axis=0)
    tangent = back[4:7] / wide(pick(ahead_norm)) + back[7:10] / wide(pick(behind_norm))
    band = back[1:4] + wide(pick(along / length)) * tangent
    speed = flat(velocity)
    mixed = wide(1.0 - mix) * speed + wide(mix * speed_norm / force_norm) * band
    kept = jnp.where(wide(reset) > 0.5, 0.0, mixed)
    movable = (image > 0) & (image < IMAGES - 1)
    speed = jnp.where(movable, kept + wide(step) * band, 0.0)
    moved = flat(pos) + wide(step) * speed
    for j in range(3):
        new_speed[j] = speed[j : j + 1]
        new_pos[j] = moved[j : j + 1]


VMEM = pl.BlockSpec(memory_space=pltpu.VMEM)
SMEM = pl.BlockSpec(memory_space=pltpu.SMEM)


def call(kernel, outs, args, scalars=(), scalar_outs=(), flops=0, limit=16 << 20):
    specs = [SMEM if i in scalars else VMEM for i in range(len(args))]
    moved = sum(a.size * a.dtype.itemsize for a in args)
    return pl.pallas_call(
        kernel,
        out_shape=[jax.ShapeDtypeStruct(s, t) for s, t in outs],
        in_specs=specs,
        out_specs=[SMEM if i in scalar_outs else VMEM for i in range(len(outs))],
        compiler_params=pltpu.CompilerParams(vmem_limit_bytes=limit),
        cost_estimate=pl.CostEstimate(flops=flops, bytes_accessed=moved, transcendentals=0),
        name=kernel.__name__,
    )(*args)


def pack_call(*args):
    return pl.pallas_call(
        pack_kernel,
        out_shape=jax.ShapeDtypeStruct((PACK_ROWS, ATOMS), BF16),
        in_specs=[pl.BlockSpec(memory_space=pltpu.HBM)] * len(args),
        out_specs=VMEM,
        scratch_shapes=[pltpu.VMEM(a.shape, a.dtype) for a in args]
        + [pltpu.SemaphoreType.DMA((len(args),))],
        compiler_params=pltpu.CompilerParams(vmem_limit_bytes=60 << 20),
        name="pack_kernel",
    )(*args)


def per_device(
    positions, velocity, embed, neighbours, send_up, send_down, climb, reset,
    filter_in, filter_out, update_weight, readout, spring, time_step, mixing,
):
    square = (ATOMS, ATOMS)
    wide = (CHANNELS, PAIRS)
    longer = (CHANNELS + EXTRA, ATOMS)
    positions = positions.transpose(1, 0, 2)
    velocity = velocity.transpose(1, 0, 2)
    packed = pack_call(
        positions, embed, neighbours.T, send_up.reshape(1, ATOMS), send_down.reshape(1, ATOMS)
    )
    pack = move(packed, TO_WORKER)
    in_t, out_t, update_t, read, settings = call(
        weights_kernel,
        [((256, 128), BF16), ((256, 128), BF16), ((256, 128), BF16), (square, F32), ((8, ATOMS), F32)],
        (
            packed, filter_in, filter_out, update_weight, readout.reshape(1, CHANNELS),
            reset, spring.reshape(1), time_step.reshape(1), mixing.reshape(1),
        ),
        scalars=(5, 6, 7, 8),
        flops=10**8,
        limit=60 << 20,
    )
    list_a, list_b, send_a, send_b = call(
        lists_kernel,
        [(square, BF16), (square, BF16), ((HALO_ROWS, ATOMS), BF16), ((HALO_ROWS + EXTRA, ATOMS), BF16)],
        (pack,),
    )
    from_b, from_a = move(send_b, SWAP_B), move(send_a, SWAP_A)
    hot, own = call(slots_kernel, [((EXT, PAIRS), BF16), ((8, ATOMS), F32)], (pack,), flops=10**9)
    hidden, send_a, send_b, update_one, pairs, rows_one = call(
        first_kernel,
        [(square, BF16), (square, BF16), (longer, BF16), (square, F32), ((8, PAIRS), F32), (wide, BF16)],
        (pack, from_a, from_b, hot, list_a, list_b, in_t, out_t, update_t),
        flops=10**9,
    )
    from_b, from_a = move(send_b, SWAP_B), move(send_a, SWAP_A)
    slope_two, filter_two = call(
        filters_kernel,
        [(wide, BF16), (wide, F32)],
        (pairs, in_t, out_t),
        flops=10**9,
    )
    energy, grad_two, rows_two, grad_own, send_a, send_b = call(
        second_kernel,
        [((8, ATOMS), F32), (square, F32), (wide, BF16), (square, F32), (square, BF16), (longer, BF16)],
        (hidden, from_a, from_b, hot, filter_two, update_t, update_weight, read),
        flops=10**9,
    )
    from_b, from_a = move(send_b, SWAP_B), move(send_a, SWAP_A)
    dsq_two, pull_one = call(
        slope_kernel,
        [((8, PAIRS), F32), (wide, F32)],
        (grad_two, rows_two, slope_two, filter_out, pairs, in_t, out_t, rows_one),
        flops=10**9,
    )
    force, send_a, send_b = call(
        third_kernel,
        [((8, ATOMS), F32), ((8, ATOMS), F32), ((8 + EXTRA, ATOMS), F32)],
        (
            grad_own, from_a, from_b, list_a, list_b, update_one, update_weight,
            pull_one, dsq_two, pairs, hot,
        ),
        flops=10**9,
    )
    from_b, from_a = move(send_b, SWAP_B), move(send_a, SWAP_A)
    (blocks,) = call(
        sums_kernel,
        [((IMAGES * 8, ATOMS), F32)],
        (force, from_a, from_b, list_a, list_b, own, energy, velocity, climb),
        scalars=(8,),
    )
    column = lax.all_to_all(blocks, AXES, 0, 0, tiled=True, axis_index_groups=COLUMNS)
    (blocks,) = call(column_kernel, [((DOMAINS * BLOCK, 2, ATOMS), F32)], (column,))
    table = lax.all_to_all(blocks, AXES, 0, 0, tiled=True, axis_index_groups=LAYERS)
    new_pos, new_speed, energies = call(
        final_kernel,
        [((3, 1, ATOMS), F32), ((3, 1, ATOMS), F32), ((1,), F32)],
        (table, positions, velocity, settings),
        scalar_outs=(2,),
    )
    return new_pos.transpose(1, 0, 2), new_speed.transpose(1, 0, 2), energies


def solution(mesh):
    placed = (
        P("image", None, "space"),
        P("image", None, "space"),
        P("space", None),
        P("space", None),
        P("space"),
        P("space"),
        P("image"),
        P("image"),
    ) + (P(),) * 7
    return jax.shard_map(
        per_device,
        mesh=mesh,
        in_specs=placed,
        out_specs=(P("image", None, "space"), P("image", None, "space"), P("image")),
        check_vma=False,
    )
```

```python
import jax
import jax.numpy as jnp
from jax import lax
from jax.experimental import pallas as pl
from jax.experimental.pallas import tpu as pltpu
from jax.sharding import PartitionSpec as P

EPSILON = 1e-06
BASIS_WIDTH = 0.6
BASIS_REACH = 6.0
BASIS = 16
IMAGES = 16
DOMAINS = 32
ATOMS = 128
CHANNELS = 128
SLOTS = 32
PAIRS = ATOMS * SLOTS
CHUNK = 2048
PER_CHUNK = CHUNK // ATOMS
CHUNKS = PAIRS // CHUNK
EXT = 3 * ATOMS
AXES = ("image", "space")
F32 = jnp.float32
BF16 = jnp.bfloat16

ROW_POS = 128
ROW_AUX = 152
ROW_NEAR = 160
PACK_ROWS = 192
HALO_ROWS = 160
EXTRA = 16
BLOCK = 5


def device_at(x, y, z, core):
    return ((y * 2 + z // 8) * 2 + core) * DOMAINS + x * 8 + z % 8


def home(image, domain):
    return image * DOMAINS + domain


RING = [
    (2, 2), (1, 2), (1, 3), (0, 3), (0, 2), (0, 1), (0, 0), (1, 0),
    (1, 1), (2, 1), (2, 0), (3, 0), (3, 1), (3, 2), (3, 3), (2, 3),
]
LAYER_PAIR = (0, 2, 3, 1)


def worker(image, domain):
    x, y = RING[domain // 2]
    home_y, half, side = image // 4, image // 2 % 2, image % 2
    return device_at(x, y, half * 8 + LAYER_PAIR[home_y] * 2 + side, domain % 2)


CELLS = [(i, d) for i in range(IMAGES) for d in range(DOMAINS)]
TO_WORKER = [(home(i, d), worker(i, d)) for i, d in CELLS]
SWAP_A = [(worker(i, d), worker(i, d ^ 1)) for i, d in CELLS]
SWAP_B = [(worker(i, d), worker(i, (d + 1) % DOMAINS if d % 2 else (d - 1) % DOMAINS)) for i, d in CELLS]
LAYERS = [[worker(i, d) for d in range(DOMAINS)] for i in range(IMAGES)]
COLUMNS = [[worker(i, d) for i in range(IMAGES)] for d in range(DOMAINS)]


def move(values, pairs):
    return lax.ppermute(values, AXES, pairs)


def place():
    image, space = lax.axis_index("image"), lax.axis_index("space")
    cell = (lax.shift_right_logical(space, 3) << 2) + lax.shift_right_logical(image, 2)
    pair = jnp.int32(0)
    for step, (x, y) in enumerate(RING):
        pair = jnp.where(cell == x * 4 + y, step, pair)
    return image, lax.shift_right_logical(image, 1) & 1, pair * 2 + (image & 1)


def dot(a, b):
    return jnp.dot(a, b, preferred_element_type=F32)


def dot_nt(a, b):
    return lax.dot_general(a, b, (((1,), (1,)), ((), ())), preferred_element_type=F32)


def gate(v):
    return 0.5 * jnp.tanh(0.5 * v) + 0.5


def halves(v):
    high = v.astype(BF16)
    return high, (v - high.astype(F32)).astype(BF16)


def thirds(v):
    high = v.astype(BF16)
    rest = v - high.astype(F32)
    middle = rest.astype(BF16)
    return high, middle, (rest - middle.astype(F32)).astype(BF16)


def centres():
    step = BASIS_REACH / (BASIS - 1)
    return lax.broadcasted_iota(jnp.int32, (BASIS, CHUNK), 0).astype(F32) * step


def stacked(v):
    high, low = halves(v)
    return jnp.concatenate([high, low, high], axis=0)


def chunk(c):
    return pl.ds(c * CHUNK, CHUNK)


def fold(v):
    total = v[:, :ATOMS]
    for k in range(1, PER_CHUNK):
        total = total + v[:, k * ATOMS : (k + 1) * ATOMS]
    return total


def spread(v):
    return jnp.concatenate([v] * PER_CHUNK, axis=1)


def flat(ref):
    return jnp.concatenate([ref[0], ref[1], ref[2]], axis=0)


def spare(ref):
    rows = ref.shape[0]
    ref[rows - EXTRA : rows, :] = jnp.zeros((EXTRA, ATOMS), ref.dtype)


def coords_of(block):
    b = block[ROW_POS : ROW_POS + 24].astype(F32)
    return b[0:8] + b[8:16] + b[16:24]


def pack_kernel(
    pos_in, embed_in, near_in, up_in, down_in, out,
    pos, embed, near, up, down, sems,
):
    pairs = ((embed_in, embed), (near_in, near), (pos_in, pos), (up_in, up), (down_in, down))
    copies = [pltpu.make_async_copy(a, b, sems.at[i]) for i, (a, b) in enumerate(pairs)]
    for copy in copies:
        copy.start()
    copies[1].wait()
    out[ROW_NEAR:PACK_ROWS, :] = (near[...].astype(F32) - float(ATOMS)).astype(BF16)
    for copy in copies[2:]:
        copy.wait()
    zeros = jnp.zeros((5, ATOMS), F32)
    parts = [jnp.concatenate([p.astype(F32), zeros], axis=0) for p in thirds(flat(pos))]
    aux = jnp.concatenate([up[...].astype(F32), down[...].astype(F32), zeros, zeros[:1]], axis=0)
    out[ROW_POS:ROW_NEAR, :] = jnp.concatenate(parts + [aux], axis=0).astype(BF16)
    copies[0].wait()
    out[0:CHANNELS, :] = embed[...].astype(F32).T.astype(BF16)


def weights_kernel(
    after, filter_in, filter_out, update, readout, reset, spring, time_step, mixing,
    in_t, out_t, update_t, read, settings,
):
    for j, value in enumerate((reset[0].astype(F32), spring[0], time_step[0], mixing[0])):
        settings[j : j + 1, :] = jnp.full((1, ATOMS), value, F32)
    settings[4:8, :] = jnp.zeros((4, ATOMS), F32)
    for l in range(2):
        rows = pl.ds(l * 128, 128)
        high, low = halves(0.5 * filter_in[l])
        filler = jnp.zeros((128 - 3 * BASIS, CHANNELS), F32)
        tall = jnp.concatenate(
            [high.astype(F32), high.astype(F32), low.astype(F32), filler], axis=0
        )
        in_t[rows, :] = tall.T.astype(BF16)
        out_t[rows, :] = filter_out[l].astype(F32).T.astype(BF16)
        update_t[rows, :] = update[l].astype(F32).T.astype(BF16)
    read[...] = jnp.broadcast_to(readout[...], (CHANNELS, ATOMS)).T


def lists_kernel(pack, list_a, list_b, send_a, send_b):
    _, _, domain = place()
    even = (domain & 1) == 0
    aux = pack[ROW_AUX : ROW_AUX + 8, :].astype(F32)
    up, down = aux[0:1], aux[1:2]
    rows = lax.broadcasted_iota(jnp.int32, (ATOMS, ATOMS), 0).astype(F32)
    block = pack[0:HALO_ROWS, :]
    for ids, chosen, send in (
        (jnp.where(even, up, down), list_a, send_a),
        (jnp.where(even, down, up), list_b, send_b),
    ):
        hot = jnp.where(rows == ids, 1.0, 0.0).astype(BF16)
        chosen[...] = hot
        send[0:HALO_ROWS, :] = dot(block, hot).astype(BF16)


    spare(send_b)


def slots_kernel(pack, hot, own):
    own[...] = coords_of(pack[0:HALO_ROWS, :])
    _, _, domain = place()
    even = (domain & 1) == 0
    slots = pack[ROW_NEAR:PACK_ROWS, :].astype(F32)
    swapped = jnp.where(slots < 0.0, slots, jnp.where(slots < 128.0, slots + 128.0, slots - 128.0))
    slots = jnp.where(even, swapped, slots)
    rows = lax.broadcasted_iota(jnp.int32, (EXT, ATOMS), 0).astype(F32) - float(ATOMS)
    for k in range(SLOTS):
        hot[:, k * ATOMS : (k + 1) * ATOMS] = jnp.where(rows == slots[k : k + 1], 1.0, 0.0).astype(BF16)


def first_kernel(
    pack, from_a, from_b, hot, list_a, list_b, in_t, out_t, update_t,
    hidden, send_a, send_b, update_one, pairs, rows_one,
):
    _, _, domain = place()
    shift = jnp.where(domain == 0, -DOMAINS, jnp.where(domain == DOMAINS - 1, DOMAINS, 0)).astype(F32)
    own = coords_of(pack[0:HALO_ROWS, :])
    first = lax.broadcasted_iota(jnp.int32, (8, ATOMS), 0) == 0
    far = coords_of(from_b[0:HALO_ROWS, :]) + jnp.where(first, shift, 0.0)
    far_rows = jnp.concatenate([p.astype(F32) for p in thirds(far)], axis=0).astype(BF16)
    ext_embed = jnp.concatenate([pack[0:CHANNELS, :], from_a[0:CHANNELS, :], from_b[0:CHANNELS, :]], axis=1)
    f32_rows = lambda ref: ref[ROW_POS:HALO_ROWS, :].astype(F32)
    far_full = jnp.concatenate([far_rows.astype(F32), jnp.zeros((8, ATOMS), F32)], axis=0)
    ext_pos = jnp.concatenate([f32_rows(pack), f32_rows(from_a), far_full], axis=1).astype(BF16)
    ext = jnp.concatenate([ext_embed, ext_pos], axis=0)
    own_wide = spread(own)
    centre = centres()
    message = jnp.zeros((CHANNELS, ATOMS), F32)
    for c in range(CHUNKS):
        got = dot(ext, hot[:, chunk(c)])
        vec = got[128:136] + got[136:144] + got[144:152] - own_wide
        pairs[:, chunk(c)] = vec
        sq = jnp.sum(vec * vec, axis=0, keepdims=True)
        scaled = (sq - centre) * (1.0 / BASIS_WIDTH)
        radial = jnp.exp(-scaled * scaled)
        half = dot(in_t[0:128, 0 : 3 * BASIS], stacked(radial))
        act = (half + half * jnp.tanh(half)).astype(BF16)
        filt = dot(out_t[0:128, :], act)
        rows = got[0:CHANNELS]
        rows_one[:, chunk(c)] = rows.astype(BF16)
        message = message + fold(filt * rows)
    upd = dot(update_t[0:128, :], message.astype(BF16))
    update_one[...] = upd
    hid = (pack[0:CHANNELS, :].astype(F32) + upd * gate(upd)).astype(BF16)
    hidden[...] = hid
    send_a[...] = dot(hid, list_a[...]).astype(BF16)
    send_b[0:CHANNELS, :] = dot(hid, list_b[...]).astype(BF16)
    spare(send_b)


def bend(pairs, in_t, layer, c, centre):
    vec = pairs[:, chunk(c)]
    sq = jnp.sum(vec * vec, axis=0, keepdims=True)
    scaled = (sq - centre) * (1.0 / BASIS_WIDTH)
    radial = jnp.exp(-scaled * scaled)
    weight = in_t[layer * 128 : (layer + 1) * 128, 0 : 3 * BASIS]
    half = dot(weight, stacked(radial))
    change = dot(weight, stacked(radial * scaled * (-2.0 / BASIS_WIDTH)))
    t = jnp.tanh(half)
    bent = half * t
    return half + bent, (1.0 + t) * (1.0 + half - bent) * change


def filters_kernel(pairs, in_t, out_t, slope_two, filter_two):
    centre = centres()
    for c in range(CHUNKS):
        act, slope = bend(pairs, in_t, 1, c, centre)
        slope_two[:, chunk(c)] = slope.astype(BF16)
        filter_two[:, chunk(c)] = dot(out_t[128:256, :], act.astype(BF16))


def second_kernel(
    hidden, from_a, from_b, hot, filter_two, update_t, update, read,
    energy, grad_two, rows_two, grad_own, grad_a, grad_b,
):
    ext = jnp.concatenate([hidden[...], from_a[...], from_b[0:CHANNELS, :]], axis=1)
    message = jnp.zeros((CHANNELS, ATOMS), F32)
    for c in range(CHUNKS):
        rows = dot(ext, hot[:, chunk(c)])
        rows_two[:, chunk(c)] = rows.astype(BF16)
        message = message + fold(filter_two[:, chunk(c)] * rows)
    upd = dot(update_t[128:256, :], message.astype(BF16))
    g = gate(upd)
    act = upd * g
    weight = read[...]
    energy[...] = jnp.broadcast_to(jnp.sum(act * weight, axis=0, keepdims=True), (8, ATOMS))
    dupd = ((g + act * (1.0 - g)) * weight).astype(BF16)
    grad = dot(update[1], dupd)
    grad_two[...] = grad
    wide = spread(grad)
    total = jnp.zeros((CHANNELS, EXT), F32)
    for c in range(CHUNKS):
        part = (filter_two[:, chunk(c)] * wide).astype(BF16)
        total = total + dot_nt(part, hot[:, chunk(c)])
    grad_own[...] = total[:, 0:ATOMS]
    grad_a[...] = total[:, ATOMS : 2 * ATOMS].astype(BF16)
    grad_b[0:CHANNELS, :] = total[:, 2 * ATOMS :].astype(BF16)
    spare(grad_b)


def slope_kernel(
    grad_two, rows_two, slope_two, filter_out, pairs, in_t, out_t, rows_one, out, pull_one
):
    centre = centres()
    wide = spread(grad_two[...].astype(BF16))
    for c in range(CHUNKS):
        dfilt = wide * rows_two[:, chunk(c)]
        dact = dot(filter_out[1], dfilt)
        part = jnp.sum(dact * slope_two[:, chunk(c)].astype(F32), axis=0, keepdims=True)
        out[:, chunk(c)] = jnp.broadcast_to(part, (8, CHUNK))
        turned = dot(out_t[0:128, :], bend(pairs, in_t, 0, c, centre)[1].astype(BF16))
        pull_one[:, chunk(c)] = turned * rows_one[:, chunk(c)].astype(F32)


def third_kernel(
    grad_own, from_a, from_b, list_a, list_b, update_one, update, pull_one, dsq_two, pairs, hot,
    force, send_a, send_b,
):
    dhidden = grad_own[...] + dot_nt(from_a[...], list_a[...]) + dot_nt(from_b[0:CHANNELS, :], list_b[...])
    upd = update_one[...]
    g = gate(upd)
    dupd = (dhidden * (g + upd * g * (1.0 - g))).astype(BF16)
    wide = spread(dot(update[0], dupd))
    own = jnp.zeros((8, ATOMS), F32)
    total = jnp.zeros((16, EXT), F32)
    for c in range(CHUNKS):
        part = jnp.sum(wide * pull_one[:, chunk(c)], axis=0, keepdims=True)
        pull = 2.0 * (part + dsq_two[:, chunk(c)]) * pairs[:, chunk(c)]
        own = own + fold(pull)
        high, low = halves(pull)
        both = jnp.concatenate([high.astype(F32), low.astype(F32)], axis=0).astype(BF16)
        total = total + dot_nt(both, hot[:, chunk(c)])
    ext = total[0:8] + total[8:16]
    force[...] = own - ext[:, 0:ATOMS]
    send_a[...] = -ext[:, ATOMS : 2 * ATOMS]
    send_b[0:8, :] = -ext[:, 2 * ATOMS :]
    spare(send_b)


def sums_kernel(force, from_a, from_b, list_a, list_b, own, energy, velocity, climb, out):
    image, _, _ = place()

    def returned(block, chosen):
        both = jnp.concatenate([p.astype(F32) for p in halves(block)], axis=0).astype(BF16)
        got = dot_nt(both, chosen)
        return got[0:8] + got[8:16]

    f = force[...] + returned(from_a[...], list_a[...]) + returned(from_b[0:8, :], list_b[...])
    speed = flat(velocity)
    movable = (image > 0) & (image < IMAGES - 1)
    speed_sq = jnp.where(movable, jnp.sum(speed * speed), 0.0)
    lane = lax.broadcasted_iota(jnp.int32, (1, ATOMS), 1)
    last = jnp.where(lane == 6 * IMAGES, speed_sq, 0.0)
    last = jnp.where(lane == 7 * IMAGES + image, climb[0].astype(F32), last)
    block = jnp.concatenate([f[0:3], own[0:3, :], energy[0:1, :], last], axis=0)
    for j in range(IMAGES):
        out[j * 8 : (j + 1) * 8, :] = block


def column_kernel(blocks, out):
    _, half, _ = place()
    part = lambda r: blocks[pl.ds(r, IMAGES, stride=8), :]
    force = [part(r) for r in range(3)]
    coords = [part(r + 3) for r in range(3)]
    ahead = [jnp.concatenate([p[1:], p[-1:]], axis=0) - p for p in coords]
    behind = [p - jnp.concatenate([p[:1], p[:-1]], axis=0) for p in coords]
    inner = lambda u, v: u[0] * v[0] + u[1] * v[1] + u[2] * v[2]
    rows = [
        part(6),
        inner(ahead, ahead),
        inner(ahead, behind),
        inner(force, ahead),
        inner(force, behind),
        inner(force, force),
        jnp.zeros((2 * IMAGES, ATOMS), F32),
    ]
    square = jnp.concatenate(rows, axis=0)
    table = jnp.sum(square.T, axis=0, keepdims=True) + jnp.sum(part(7), axis=0, keepdims=True)
    parts = force + ahead + behind
    for y in range(4):
        for core in range(2):
            low = y * 4 + core
            pick = lambda v: jnp.where(half == 0, v[low : low + 1], v[low + 2 : low + 3])
            lines = [table] + [pick(v) for v in parts]
            pairs = [jnp.concatenate(lines[2 * r : 2 * r + 2], axis=0) for r in range(BLOCK)]
            for x in range(4):
                target = RING.index((x, y)) * 2 + core
                for r in range(BLOCK):
                    out[target * BLOCK + r] = pairs[r]


def final_kernel(blocks, pos, velocity, settings, new_pos, new_speed, energy):
    image, _, _ = place()
    space = lax.axis_index("space")
    reset, spring, step, mix = (settings[j : j + 1, :] for j in range(4))
    total = blocks[0]
    for j in range(1, DOMAINS):
        total = total + blocks[j * BLOCK]
    row = lax.broadcasted_iota(jnp.int32, (IMAGES, 1), 0)
    lane = lax.broadcasted_iota(jnp.int32, (IMAGES, ATOMS), 1)
    table = jnp.broadcast_to(total[0:1], (IMAGES, ATOMS))
    column = lambda j: jnp.sum(jnp.where(lane == row + j * IMAGES, table, 0.0), axis=1, keepdims=True)
    e, a, ab, fa, fb, ff, vv, level = (column(j) for j in range(8))
    b = jnp.concatenate([a[:1], a[:-1]], axis=0)
    down = lambda v: jnp.sum(v, axis=0, keepdims=True)
    ahead_norm = jnp.sqrt(a + EPSILON)
    behind_norm = jnp.sqrt(b + EPSILON)
    tangent_sq = jnp.maximum(
        a / (ahead_norm * ahead_norm)
        + b / (behind_norm * behind_norm)
        + 2.0 * ab / (ahead_norm * behind_norm),
        0.0,
    )
    length = jnp.sqrt(tangent_sq + EPSILON)
    unit_sq = tangent_sq / (tangent_sq + EPSILON)
    parallel = (fa / ahead_norm + fb / behind_norm) / length
    tension = spring[:, 0:1] * (ahead_norm - behind_norm)
    along = jnp.where(level > 0.5, -2.0 * parallel, tension - parallel)
    band_sq = ff + 2.0 * along * parallel + along * along * unit_sq
    inner = (row > 0) & (row < IMAGES - 1)
    force_norm = jnp.sqrt(down(jnp.where(inner, jnp.maximum(band_sq, 0.0), 0.0)) + EPSILON)
    speed_norm = jnp.sqrt(down(vv) + EPSILON)
    mine = row == image
    pick = lambda v: down(jnp.where(mine, v, 0.0))
    wide = lambda v: jnp.broadcast_to(jnp.broadcast_to(v, (1, ATOMS)), (3, ATOMS))
    energy[0] = jnp.sum(jnp.where(mine, e, 0.0))
    back = jnp.concatenate([blocks[space * BLOCK + r] for r in range(BLOCK)], axis=0)
    tangent = back[4:7] / wide(pick(ahead_norm)) + back[7:10] / wide(pick(behind_norm))
    band = back[1:4] + wide(pick(along / length)) * tangent
    speed = flat(velocity)
    mixed = wide(1.0 - mix) * speed + wide(mix * speed_norm / force_norm) * band
    kept = jnp.where(wide(reset) > 0.5, 0.0, mixed)
    movable = (image > 0) & (image < IMAGES - 1)
    speed = jnp.where(movable, kept + wide(step) * band, 0.0)
    moved = flat(pos) + wide(step) * speed
    for j in range(3):
        new_speed[j] = speed[j : j + 1]
        new_pos[j] = moved[j : j + 1]


VMEM = pl.BlockSpec(memory_space=pltpu.VMEM)
SMEM = pl.BlockSpec(memory_space=pltpu.SMEM)


def call(kernel, outs, args, scalars=(), scalar_outs=(), flops=0, limit=16 << 20):
    specs = [SMEM if i in scalars else VMEM for i in range(len(args))]
    moved = sum(a.size * a.dtype.itemsize for a in args)
    return pl.pallas_call(
        kernel,
        out_shape=[jax.ShapeDtypeStruct(s, t) for s, t in outs],
        in_specs=specs,
        out_specs=[SMEM if i in scalar_outs else VMEM for i in range(len(outs))],
        compiler_params=pltpu.CompilerParams(vmem_limit_bytes=limit),
        cost_estimate=pl.CostEstimate(flops=flops, bytes_accessed=moved, transcendentals=0),
        name=kernel.__name__,
    )(*args)


def pack_call(*args):
    return pl.pallas_call(
        pack_kernel,
        out_shape=jax.ShapeDtypeStruct((PACK_ROWS, ATOMS), BF16),
        in_specs=[pl.BlockSpec(memory_space=pltpu.HBM)] * len(args),
        out_specs=VMEM,
        scratch_shapes=[pltpu.VMEM(a.shape, a.dtype) for a in args]
        + [pltpu.SemaphoreType.DMA((len(args),))],
        compiler_params=pltpu.CompilerParams(vmem_limit_bytes=60 << 20),
        name="pack_kernel",
    )(*args)


def per_device(
    positions, velocity, embed, neighbours, send_up, send_down, climb, reset,
    filter_in, filter_out, update_weight, readout, spring, time_step, mixing,
):
    square = (ATOMS, ATOMS)
    wide = (CHANNELS, PAIRS)
    longer = (CHANNELS + EXTRA, ATOMS)
    positions = positions.transpose(1, 0, 2)
    velocity = velocity.transpose(1, 0, 2)
    packed = pack_call(
        positions, embed, neighbours.T, send_up.reshape(1, ATOMS), send_down.reshape(1, ATOMS)
    )
    pack = move(packed, TO_WORKER)
    in_t, out_t, update_t, read, settings = call(
        weights_kernel,
        [((256, 128), BF16), ((256, 128), BF16), ((256, 128), BF16), (square, F32), ((8, ATOMS), F32)],
        (
            packed, filter_in, filter_out, update_weight, readout.reshape(1, CHANNELS),
            reset, spring.reshape(1), time_step.reshape(1), mixing.reshape(1),
        ),
        scalars=(5, 6, 7, 8),
        flops=10**8,
        limit=60 << 20,
    )
    list_a, list_b, send_a, send_b = call(
        lists_kernel,
        [(square, BF16), (square, BF16), ((HALO_ROWS, ATOMS), BF16), ((HALO_ROWS + EXTRA, ATOMS), BF16)],
        (pack,),
    )
    from_b, from_a = move(send_b, SWAP_B), move(send_a, SWAP_A)
    hot, own = call(slots_kernel, [((EXT, PAIRS), BF16), ((8, ATOMS), F32)], (pack,), flops=10**9)
    hidden, send_a, send_b, update_one, pairs, rows_one = call(
        first_kernel,
        [(square, BF16), (square, BF16), (longer, BF16), (square, F32), ((8, PAIRS), F32), (wide, BF16)],
        (pack, from_a, from_b, hot, list_a, list_b, in_t, out_t, update_t),
        flops=10**9,
    )
    from_b, from_a = move(send_b, SWAP_B), move(send_a, SWAP_A)
    slope_two, filter_two = call(
        filters_kernel,
        [(wide, BF16), (wide, F32)],
        (pairs, in_t, out_t),
        flops=10**9,
    )
    energy, grad_two, rows_two, grad_own, send_a, send_b = call(
        second_kernel,
        [((8, ATOMS), F32), (square, F32), (wide, BF16), (square, F32), (square, BF16), (longer, BF16)],
        (hidden, from_a, from_b, hot, filter_two, update_t, update_weight, read),
        flops=10**9,
    )
    from_b, from_a = move(send_b, SWAP_B), move(send_a, SWAP_A)
    dsq_two, pull_one = call(
        slope_kernel,
        [((8, PAIRS), F32), (wide, F32)],
        (grad_two, rows_two, slope_two, filter_out, pairs, in_t, out_t, rows_one),
        flops=10**9,
    )
    force, send_a, send_b = call(
        third_kernel,
        [((8, ATOMS), F32), ((8, ATOMS), F32), ((8 + EXTRA, ATOMS), F32)],
        (
            grad_own, from_a, from_b, list_a, list_b, update_one, update_weight,
            pull_one, dsq_two, pairs, hot,
        ),
        flops=10**9,
    )
    from_b, from_a = move(send_b, SWAP_B), move(send_a, SWAP_A)
    (blocks,) = call(
        sums_kernel,
        [((IMAGES * 8, ATOMS), F32)],
        (force, from_a, from_b, list_a, list_b, own, energy, velocity, climb),
        scalars=(8,),
    )
    column = lax.all_to_all(blocks, AXES, 0, 0, tiled=True, axis_index_groups=COLUMNS)
    (blocks,) = call(column_kernel, [((DOMAINS * BLOCK, 2, ATOMS), F32)], (column,))
    table = lax.all_to_all(blocks, AXES, 0, 0, tiled=True, axis_index_groups=LAYERS)
    new_pos, new_speed, energies = call(
        final_kernel,
        [((3, 1, ATOMS), F32), ((3, 1, ATOMS), F32), ((1,), F32)],
        (table, positions, velocity, settings),
        scalar_outs=(2,),
    )
    return new_pos.transpose(1, 0, 2), new_speed.transpose(1, 0, 2), energies


def solution(mesh):
    placed = (
        P("image", None, "space"),
        P("image", None, "space"),
        P("space", None),
        P("space", None),
        P("space"),
        P("space"),
        P("image"),
        P("image"),
    ) + (P(),) * 7
    return jax.shard_map(
        per_device,
        mesh=mesh,
        in_specs=placed,
        out_specs=(P("image", None, "space"), P("image", None, "space"), P("image")),
        check_vma=False,
    )
```

```python
import jax
import jax.numpy as jnp
from jax import lax
from jax.experimental import pallas as pl
from jax.experimental.pallas import tpu as pltpu
from jax.sharding import PartitionSpec as P

EPSILON = 1e-06
BASIS_WIDTH = 0.6
BASIS_REACH = 6.0
BASIS = 16
IMAGES = 16
DOMAINS = 32
ATOMS = 128
CHANNELS = 128
SLOTS = 32
PAIRS = ATOMS * SLOTS
CHUNK = 2048
PER_CHUNK = CHUNK // ATOMS
CHUNKS = PAIRS // CHUNK
EXT = 3 * ATOMS
AXES = ("image", "space")
F32 = jnp.float32
BF16 = jnp.bfloat16

ROW_POS = 128
ROW_AUX = 152
ROW_NEAR = 160
PACK_ROWS = 192
HALO_ROWS = 160
EXTRA = 16
BLOCK = 5


def device_at(x, y, z, core):
    return ((y * 2 + z // 8) * 2 + core) * DOMAINS + x * 8 + z % 8


def home(image, domain):
    return image * DOMAINS + domain


RING = [
    (2, 2), (1, 2), (1, 3), (0, 3), (0, 2), (0, 1), (0, 0), (1, 0),
    (1, 1), (2, 1), (2, 0), (3, 0), (3, 1), (3, 2), (3, 3), (2, 3),
]
LAYER_PAIR = (0, 2, 3, 1)


def worker(image, domain):
    x, y = RING[domain // 2]
    home_y, half, side = image // 4, image // 2 % 2, image % 2
    return device_at(x, y, half * 8 + LAYER_PAIR[home_y] * 2 + side, domain % 2)


CELLS = [(i, d) for i in range(IMAGES) for d in range(DOMAINS)]
TO_WORKER = [(home(i, d), worker(i, d)) for i, d in CELLS]
SWAP_A = [(worker(i, d), worker(i, d ^ 1)) for i, d in CELLS]
SWAP_B = [(worker(i, d), worker(i, (d + 1) % DOMAINS if d % 2 else (d - 1) % DOMAINS)) for i, d in CELLS]
LAYERS = [[worker(i, d) for d in range(DOMAINS)] for i in range(IMAGES)]
COLUMNS = [[worker(i, d) for i in range(IMAGES)] for d in range(DOMAINS)]


def move(values, pairs):
    return lax.ppermute(values, AXES, pairs)


def place():
    image, space = lax.axis_index("image"), lax.axis_index("space")
    cell = (lax.shift_right_logical(space, 3) << 2) + lax.shift_right_logical(image, 2)
    pair = jnp.int32(0)
    for step, (x, y) in enumerate(RING):
        pair = jnp.where(cell == x * 4 + y, step, pair)
    return image, lax.shift_right_logical(image, 1) & 1, pair * 2 + (image & 1)


def dot(a, b):
    return jnp.dot(a, b, preferred_element_type=F32)


def dot_nt(a, b):
    return lax.dot_general(a, b, (((1,), (1,)), ((), ())), preferred_element_type=F32)


def gate(v):
    return 0.5 * jnp.tanh(0.5 * v) + 0.5


def halves(v):
    high = v.astype(BF16)
    return high, (v - high.astype(F32)).astype(BF16)


def thirds(v):
    high = v.astype(BF16)
    rest = v - high.astype(F32)
    middle = rest.astype(BF16)
    return high, middle, (rest - middle.astype(F32)).astype(BF16)


def centres():
    step = BASIS_REACH / (BASIS - 1)
    return lax.broadcasted_iota(jnp.int32, (BASIS, CHUNK), 0).astype(F32) * step


def stacked(v):
    high, low = halves(v)
    return jnp.concatenate([high, low, high], axis=0)


def chunk(c):
    return pl.ds(c * CHUNK, CHUNK)


def fold(v):
    total = v[:, :ATOMS]
    for k in range(1, PER_CHUNK):
        total = total + v[:, k * ATOMS : (k + 1) * ATOMS]
    return total


def spread(v):
    return jnp.concatenate([v] * PER_CHUNK, axis=1)


def flat(ref):
    return jnp.concatenate([ref[0], ref[1], ref[2]], axis=0)


def spare(ref):
    rows = ref.shape[0]
    ref[rows - EXTRA : rows, :] = jnp.zeros((EXTRA, ATOMS), ref.dtype)


def coords_of(block):
    b = block[ROW_POS : ROW_POS + 24].astype(F32)
    return b[0:8] + b[8:16] + b[16:24]


def pack_kernel(
    pos_in, embed_in, near_in, up_in, down_in, out,
    pos, embed, near, up, down, sems,
):
    pairs = ((embed_in, embed), (near_in, near), (pos_in, pos), (up_in, up), (down_in, down))
    copies = [pltpu.make_async_copy(a, b, sems.at[i]) for i, (a, b) in enumerate(pairs)]
    for copy in copies:
        copy.start()
    copies[1].wait()
    out[ROW_NEAR:PACK_ROWS, :] = (near[...].astype(F32) - float(ATOMS)).astype(BF16)
    for copy in copies[2:]:
        copy.wait()
    zeros = jnp.zeros((5, ATOMS), F32)
    parts = [jnp.concatenate([p.astype(F32), zeros], axis=0) for p in thirds(flat(pos))]
    aux = jnp.concatenate([up[...].astype(F32), down[...].astype(F32), zeros, zeros[:1]], axis=0)
    out[ROW_POS:ROW_NEAR, :] = jnp.concatenate(parts + [aux], axis=0).astype(BF16)
    copies[0].wait()
    out[0:CHANNELS, :] = embed[...].astype(F32).T.astype(BF16)


def weights_kernel(
    after, filter_in, filter_out, update, readout, reset, spring, time_step, mixing, climb,
    in_t, out_t, update_t, read, settings,
):
    values = (reset[0].astype(F32), spring[0], time_step[0], mixing[0], climb[0].astype(F32))
    for j, value in enumerate(values):
        settings[j : j + 1, :] = jnp.full((1, ATOMS), value, F32)
    settings[5:8, :] = jnp.zeros((3, ATOMS), F32)
    for l in range(2):
        rows = pl.ds(l * 128, 128)
        high, low = halves(0.5 * filter_in[l])
        filler = jnp.zeros((128 - 3 * BASIS, CHANNELS), F32)
        tall = jnp.concatenate(
            [high.astype(F32), high.astype(F32), low.astype(F32), filler], axis=0
        )
        in_t[rows, :] = tall.T.astype(BF16)
        out_t[rows, :] = filter_out[l].astype(F32).T.astype(BF16)
        update_t[rows, :] = update[l].astype(F32).T.astype(BF16)
    read[...] = jnp.broadcast_to(readout[...], (CHANNELS, ATOMS)).T


def lists_kernel(pack, list_a, list_b, send_a, send_b):
    _, _, domain = place()
    even = (domain & 1) == 0
    aux = pack[ROW_AUX : ROW_AUX + 8, :].astype(F32)
    up, down = aux[0:1], aux[1:2]
    rows = lax.broadcasted_iota(jnp.int32, (ATOMS, ATOMS), 0).astype(F32)
    block = pack[0:HALO_ROWS, :]
    for ids, chosen, send in (
        (jnp.where(even, up, down), list_a, send_a),
        (jnp.where(even, down, up), list_b, send_b),
    ):
        hot = jnp.where(rows == ids, 1.0, 0.0).astype(BF16)
        chosen[...] = hot
        send[0:HALO_ROWS, :] = dot(block, hot).astype(BF16)


    spare(send_b)


def slots_kernel(pack, hot, own):
    own[...] = coords_of(pack[0:HALO_ROWS, :])
    _, _, domain = place()
    even = (domain & 1) == 0
    slots = pack[ROW_NEAR:PACK_ROWS, :].astype(F32)
    swapped = jnp.where(slots < 0.0, slots, jnp.where(slots < 128.0, slots + 128.0, slots - 128.0))
    slots = jnp.where(even, swapped, slots)
    rows = lax.broadcasted_iota(jnp.int32, (EXT, ATOMS), 0).astype(F32) - float(ATOMS)
    for k in range(SLOTS):
        hot[:, k * ATOMS : (k + 1) * ATOMS] = jnp.where(rows == slots[k : k + 1], 1.0, 0.0).astype(BF16)


def first_kernel(
    pack, from_a, from_b, hot, list_a, list_b, in_t, out_t, update_t,
    hidden, send_a, send_b, update_one, pairs, rows_one,
):
    _, _, domain = place()
    shift = jnp.where(domain == 0, -DOMAINS, jnp.where(domain == DOMAINS - 1, DOMAINS, 0)).astype(F32)
    own = coords_of(pack[0:HALO_ROWS, :])
    first = lax.broadcasted_iota(jnp.int32, (8, ATOMS), 0) == 0
    far = coords_of(from_b[0:HALO_ROWS, :]) + jnp.where(first, shift, 0.0)
    far_rows = jnp.concatenate([p.astype(F32) for p in thirds(far)], axis=0).astype(BF16)
    ext_embed = jnp.concatenate([pack[0:CHANNELS, :], from_a[0:CHANNELS, :], from_b[0:CHANNELS, :]], axis=1)
    f32_rows = lambda ref: ref[ROW_POS:HALO_ROWS, :].astype(F32)
    far_full = jnp.concatenate([far_rows.astype(F32), jnp.zeros((8, ATOMS), F32)], axis=0)
    ext_pos = jnp.concatenate([f32_rows(pack), f32_rows(from_a), far_full], axis=1).astype(BF16)
    ext = jnp.concatenate([ext_embed, ext_pos], axis=0)
    own_wide = spread(own)
    centre = centres()
    message = jnp.zeros((CHANNELS, ATOMS), F32)
    for c in range(CHUNKS):
        got = dot(ext, hot[:, chunk(c)])
        vec = got[128:136] + got[136:144] + got[144:152] - own_wide
        pairs[:, chunk(c)] = vec
        sq = jnp.sum(vec * vec, axis=0, keepdims=True)
        scaled = (sq - centre) * (1.0 / BASIS_WIDTH)
        radial = jnp.exp(-scaled * scaled)
        half = dot(in_t[0:128, 0 : 3 * BASIS], stacked(radial))
        act = (half + half * jnp.tanh(half)).astype(BF16)
        filt = dot(out_t[0:128, :], act)
        rows = got[0:CHANNELS]
        rows_one[:, chunk(c)] = rows.astype(BF16)
        message = message + fold(filt * rows)
    upd = dot(update_t[0:128, :], message.astype(BF16))
    update_one[...] = upd
    hid = (pack[0:CHANNELS, :].astype(F32) + upd * gate(upd)).astype(BF16)
    hidden[...] = hid
    send_a[...] = dot(hid, list_a[...]).astype(BF16)
    send_b[0:CHANNELS, :] = dot(hid, list_b[...]).astype(BF16)
    spare(send_b)


def bend(pairs, in_t, layer, c, centre):
    vec = pairs[:, chunk(c)]
    sq = jnp.sum(vec * vec, axis=0, keepdims=True)
    scaled = (sq - centre) * (1.0 / BASIS_WIDTH)
    radial = jnp.exp(-scaled * scaled)
    weight = in_t[layer * 128 : (layer + 1) * 128, 0 : 3 * BASIS]
    half = dot(weight, stacked(radial))
    change = dot(weight, stacked(radial * scaled * (-2.0 / BASIS_WIDTH)))
    t = jnp.tanh(half)
    bent = half * t
    return half + bent, (1.0 + t) * (1.0 + half - bent) * change


def filters_kernel(pairs, in_t, out_t, slope_two, filter_two):
    centre = centres()
    for c in range(CHUNKS):
        act, slope = bend(pairs, in_t, 1, c, centre)
        slope_two[:, chunk(c)] = slope.astype(BF16)
        filter_two[:, chunk(c)] = dot(out_t[128:256, :], act.astype(BF16))


def second_kernel(
    hidden, from_a, from_b, hot, filter_two, update_t, update, read,
    energy, grad_two, rows_two, grad_own, grad_a, grad_b,
):
    ext = jnp.concatenate([hidden[...], from_a[...], from_b[0:CHANNELS, :]], axis=1)
    message = jnp.zeros((CHANNELS, ATOMS), F32)
    for c in range(CHUNKS):
        rows = dot(ext, hot[:, chunk(c)])
        rows_two[:, chunk(c)] = rows.astype(BF16)
        message = message + fold(filter_two[:, chunk(c)] * rows)
    upd = dot(update_t[128:256, :], message.astype(BF16))
    g = gate(upd)
    act = upd * g
    weight = read[...]
    energy[...] = jnp.broadcast_to(jnp.sum(act * weight, axis=0, keepdims=True), (8, ATOMS))
    dupd = ((g + act * (1.0 - g)) * weight).astype(BF16)
    grad = dot(update[1], dupd)
    grad_two[...] = grad
    wide = spread(grad)
    total = jnp.zeros((CHANNELS, EXT), F32)
    for c in range(CHUNKS):
        part = (filter_two[:, chunk(c)] * wide).astype(BF16)
        total = total + dot_nt(part, hot[:, chunk(c)])
    grad_own[...] = total[:, 0:ATOMS]
    grad_a[...] = total[:, ATOMS : 2 * ATOMS].astype(BF16)
    grad_b[0:CHANNELS, :] = total[:, 2 * ATOMS :].astype(BF16)
    spare(grad_b)


def slope_kernel(
    grad_two, rows_two, slope_two, filter_out, pairs, in_t, out_t, rows_one, out, pull_one
):
    centre = centres()
    wide = spread(grad_two[...].astype(BF16))
    for c in range(CHUNKS):
        dfilt = wide * rows_two[:, chunk(c)]
        dact = dot(filter_out[1], dfilt)
        part = jnp.sum(dact * slope_two[:, chunk(c)].astype(F32), axis=0, keepdims=True)
        out[:, chunk(c)] = jnp.broadcast_to(part, (8, CHUNK))
        turned = dot(out_t[0:128, :], bend(pairs, in_t, 0, c, centre)[1].astype(BF16))
        pull_one[:, chunk(c)] = turned * rows_one[:, chunk(c)].astype(F32)


def third_kernel(
    grad_own, from_a, from_b, list_a, list_b, update_one, update, pull_one, dsq_two, pairs, hot,
    force, send_a, send_b,
):
    dhidden = grad_own[...] + dot_nt(from_a[...], list_a[...]) + dot_nt(from_b[0:CHANNELS, :], list_b[...])
    upd = update_one[...]
    g = gate(upd)
    dupd = (dhidden * (g + upd * g * (1.0 - g))).astype(BF16)
    wide = spread(dot(update[0], dupd))
    own = jnp.zeros((8, ATOMS), F32)
    total = jnp.zeros((16, EXT), F32)
    for c in range(CHUNKS):
        part = jnp.sum(wide * pull_one[:, chunk(c)], axis=0, keepdims=True)
        pull = 2.0 * (part + dsq_two[:, chunk(c)]) * pairs[:, chunk(c)]
        own = own + fold(pull)
        high, low = halves(pull)
        both = jnp.concatenate([high.astype(F32), low.astype(F32)], axis=0).astype(BF16)
        total = total + dot_nt(both, hot[:, chunk(c)])
    ext = total[0:8] + total[8:16]
    force[...] = own - ext[:, 0:ATOMS]
    send_a[...] = -ext[:, ATOMS : 2 * ATOMS]
    send_b[0:8, :] = -ext[:, 2 * ATOMS :]
    spare(send_b)


def sums_kernel(force, from_a, from_b, list_a, list_b, own, energy, velocity, settings, out):
    image, _, _ = place()

    def returned(block, chosen):
        both = jnp.concatenate([p.astype(F32) for p in halves(block)], axis=0).astype(BF16)
        got = dot_nt(both, chosen)
        return got[0:8] + got[8:16]

    f = force[...] + returned(from_a[...], list_a[...]) + returned(from_b[0:8, :], list_b[...])
    speed = flat(velocity)
    movable = (image > 0) & (image < IMAGES - 1)
    speed_sq = jnp.where(movable, jnp.sum(speed * speed), 0.0)
    lane = lax.broadcasted_iota(jnp.int32, (1, ATOMS), 1)
    last = jnp.where(lane == 6 * IMAGES, speed_sq, 0.0)
    last = jnp.where(lane == 7 * IMAGES + image, settings[4:5, :], last)
    block = jnp.concatenate([f[0:3], own[0:3, :], energy[0:1, :], last], axis=0)
    for j in range(IMAGES):
        out[j * 8 : (j + 1) * 8, :] = block


def column_kernel(blocks, out):
    _, half, _ = place()
    part = lambda r: blocks[pl.ds(r, IMAGES, stride=8), :]
    force = [part(r) for r in range(3)]
    coords = [part(r + 3) for r in range(3)]
    ahead = [jnp.concatenate([p[1:], p[-1:]], axis=0) - p for p in coords]
    behind = [p - jnp.concatenate([p[:1], p[:-1]], axis=0) for p in coords]
    inner = lambda u, v: u[0] * v[0] + u[1] * v[1] + u[2] * v[2]
    rows = [
        part(6),
        inner(ahead, ahead),
        inner(ahead, behind),
        inner(force, ahead),
        inner(force, behind),
        inner(force, force),
        jnp.zeros((2 * IMAGES, ATOMS), F32),
    ]
    square = jnp.concatenate(rows, axis=0)
    table = jnp.sum(square.T, axis=0, keepdims=True) + jnp.sum(part(7), axis=0, keepdims=True)
    parts = force + ahead + behind
    for y in range(4):
        for core in range(2):
            low = y * 4 + core
            pick = lambda v: jnp.where(half == 0, v[low : low + 1], v[low + 2 : low + 3])
            lines = [table] + [pick(v) for v in parts]
            pairs = [jnp.concatenate(lines[2 * r : 2 * r + 2], axis=0) for r in range(BLOCK)]
            for x in range(4):
                target = RING.index((x, y)) * 2 + core
                for r in range(BLOCK):
                    out[target * BLOCK + r] = pairs[r]


def final_kernel(blocks, pos, velocity, settings, new_pos, new_speed, energy):
    image, _, _ = place()
    space = lax.axis_index("space")
    reset, spring, step, mix = (settings[j : j + 1, :] for j in range(4))
    total = blocks[0]
    for j in range(1, DOMAINS):
        total = total + blocks[j * BLOCK]
    row = lax.broadcasted_iota(jnp.int32, (IMAGES, 1), 0)
    lane = lax.broadcasted_iota(jnp.int32, (IMAGES, ATOMS), 1)
    table = jnp.broadcast_to(total[0:1], (IMAGES, ATOMS))
    column = lambda j: jnp.sum(jnp.where(lane == row + j * IMAGES, table, 0.0), axis=1, keepdims=True)
    e, a, ab, fa, fb, ff, vv, level = (column(j) for j in range(8))
    b = jnp.concatenate([a[:1], a[:-1]], axis=0)
    down = lambda v: jnp.sum(v, axis=0, keepdims=True)
    ahead_norm = jnp.sqrt(a + EPSILON)
    behind_norm = jnp.sqrt(b + EPSILON)
    tangent_sq = jnp.maximum(
        a / (ahead_norm * ahead_norm)
        + b / (behind_norm * behind_norm)
        + 2.0 * ab / (ahead_norm * behind_norm),
        0.0,
    )
    length = jnp.sqrt(tangent_sq + EPSILON)
    unit_sq = tangent_sq / (tangent_sq + EPSILON)
    parallel = (fa / ahead_norm + fb / behind_norm) / length
    tension = spring[:, 0:1] * (ahead_norm - behind_norm)
    along = jnp.where(level > 0.5, -2.0 * parallel, tension - parallel)
    band_sq = ff + 2.0 * along * parallel + along * along * unit_sq
    inner = (row > 0) & (row < IMAGES - 1)
    force_norm = jnp.sqrt(down(jnp.where(inner, jnp.maximum(band_sq, 0.0), 0.0)) + EPSILON)
    speed_norm = jnp.sqrt(down(vv) + EPSILON)
    mine = row == image
    pick = lambda v: down(jnp.where(mine, v, 0.0))
    wide = lambda v: jnp.broadcast_to(jnp.broadcast_to(v, (1, ATOMS)), (3, ATOMS))
    energy[0] = jnp.sum(jnp.where(mine, e, 0.0))
    back = jnp.concatenate([blocks[space * BLOCK + r] for r in range(BLOCK)], axis=0)
    tangent = back[4:7] / wide(pick(ahead_norm)) + back[7:10] / wide(pick(behind_norm))
    band = back[1:4] + wide(pick(along / length)) * tangent
    speed = flat(velocity)
    mixed = wide(1.0 - mix) * speed + wide(mix * speed_norm / force_norm) * band
    kept = jnp.where(wide(reset) > 0.5, 0.0, mixed)
    movable = (image > 0) & (image < IMAGES - 1)
    speed = jnp.where(movable, kept + wide(step) * band, 0.0)
    moved = flat(pos) + wide(step) * speed
    for j in range(3):
        new_speed[j] = speed[j : j + 1]
        new_pos[j] = moved[j : j + 1]


VMEM = pl.BlockSpec(memory_space=pltpu.VMEM)
SMEM = pl.BlockSpec(memory_space=pltpu.SMEM)


def call(kernel, outs, args, scalars=(), scalar_outs=(), flops=0, limit=16 << 20):
    specs = [SMEM if i in scalars else VMEM for i in range(len(args))]
    moved = sum(a.size * a.dtype.itemsize for a in args)
    return pl.pallas_call(
        kernel,
        out_shape=[jax.ShapeDtypeStruct(s, t) for s, t in outs],
        in_specs=specs,
        out_specs=[SMEM if i in scalar_outs else VMEM for i in range(len(outs))],
        compiler_params=pltpu.CompilerParams(vmem_limit_bytes=limit),
        cost_estimate=pl.CostEstimate(flops=flops, bytes_accessed=moved, transcendentals=0),
        name=kernel.__name__,
    )(*args)


def pack_call(*args):
    return pl.pallas_call(
        pack_kernel,
        out_shape=jax.ShapeDtypeStruct((PACK_ROWS, ATOMS), BF16),
        in_specs=[pl.BlockSpec(memory_space=pltpu.HBM)] * len(args),
        out_specs=VMEM,
        scratch_shapes=[pltpu.VMEM(a.shape, a.dtype) for a in args]
        + [pltpu.SemaphoreType.DMA((len(args),))],
        compiler_params=pltpu.CompilerParams(vmem_limit_bytes=60 << 20),
        name="pack_kernel",
    )(*args)


def per_device(
    positions, velocity, embed, neighbours, send_up, send_down, climb, reset,
    filter_in, filter_out, update_weight, readout, spring, time_step, mixing,
):
    square = (ATOMS, ATOMS)
    wide = (CHANNELS, PAIRS)
    longer = (CHANNELS + EXTRA, ATOMS)
    positions = positions.transpose(1, 0, 2)
    velocity = velocity.transpose(1, 0, 2)
    packed = pack_call(
        positions, embed, neighbours.T, send_up.reshape(1, ATOMS), send_down.reshape(1, ATOMS)
    )
    pack = move(packed, TO_WORKER)
    in_t, out_t, update_t, read, settings = call(
        weights_kernel,
        [((256, 128), BF16), ((256, 128), BF16), ((256, 128), BF16), (square, F32), ((8, ATOMS), F32)],
        (
            packed, filter_in, filter_out, update_weight, readout.reshape(1, CHANNELS),
            reset, spring.reshape(1), time_step.reshape(1), mixing.reshape(1), climb,
        ),
        scalars=(5, 6, 7, 8, 9),
        flops=10**8,
        limit=60 << 20,
    )
    list_a, list_b, send_a, send_b = call(
        lists_kernel,
        [(square, BF16), (square, BF16), ((HALO_ROWS, ATOMS), BF16), ((HALO_ROWS + EXTRA, ATOMS), BF16)],
        (pack,),
    )
    from_b, from_a = move(send_b, SWAP_B), move(send_a, SWAP_A)
    hot, own = call(slots_kernel, [((EXT, PAIRS), BF16), ((8, ATOMS), F32)], (pack,), flops=10**9)
    hidden, send_a, send_b, update_one, pairs, rows_one = call(
        first_kernel,
        [(square, BF16), (square, BF16), (longer, BF16), (square, F32), ((8, PAIRS), F32), (wide, BF16)],
        (pack, from_a, from_b, hot, list_a, list_b, in_t, out_t, update_t),
        flops=10**9,
    )
    from_b, from_a = move(send_b, SWAP_B), move(send_a, SWAP_A)
    slope_two, filter_two = call(
        filters_kernel,
        [(wide, BF16), (wide, F32)],
        (pairs, in_t, out_t),
        flops=10**9,
    )
    energy, grad_two, rows_two, grad_own, send_a, send_b = call(
        second_kernel,
        [((8, ATOMS), F32), (square, F32), (wide, BF16), (square, F32), (square, BF16), (longer, BF16)],
        (hidden, from_a, from_b, hot, filter_two, update_t, update_weight, read),
        flops=10**9,
    )
    from_b, from_a = move(send_b, SWAP_B), move(send_a, SWAP_A)
    dsq_two, pull_one = call(
        slope_kernel,
        [((8, PAIRS), F32), (wide, F32)],
        (grad_two, rows_two, slope_two, filter_out, pairs, in_t, out_t, rows_one),
        flops=10**9,
    )
    force, send_a, send_b = call(
        third_kernel,
        [((8, ATOMS), F32), ((8, ATOMS), F32), ((8 + EXTRA, ATOMS), F32)],
        (
            grad_own, from_a, from_b, list_a, list_b, update_one, update_weight,
            pull_one, dsq_two, pairs, hot,
        ),
        flops=10**9,
    )
    from_b, from_a = move(send_b, SWAP_B), move(send_a, SWAP_A)
    (blocks,) = call(
        sums_kernel,
        [((IMAGES * 8, ATOMS), F32)],
        (force, from_a, from_b, list_a, list_b, own, energy, velocity, settings),
    )
    column = lax.all_to_all(blocks, AXES, 0, 0, tiled=True, axis_index_groups=COLUMNS)
    (blocks,) = call(column_kernel, [((DOMAINS * BLOCK, 2, ATOMS), F32)], (column,))
    table = lax.all_to_all(blocks, AXES, 0, 0, tiled=True, axis_index_groups=LAYERS)
    new_pos, new_speed, energies = call(
        final_kernel,
        [((3, 1, ATOMS), F32), ((3, 1, ATOMS), F32), ((1,), F32)],
        (table, positions, velocity, settings),
        scalar_outs=(2,),
    )
    return new_pos.transpose(1, 0, 2), new_speed.transpose(1, 0, 2), energies


def solution(mesh):
    placed = (
        P("image", None, "space"),
        P("image", None, "space"),
        P("space", None),
        P("space", None),
        P("space"),
        P("space"),
        P("image"),
        P("image"),
    ) + (P(),) * 7
    return jax.shard_map(
        per_device,
        mesh=mesh,
        in_specs=placed,
        out_specs=(P("image", None, "space"), P("image", None, "space"), P("image")),
        check_vma=False,
    )
```
